32 devices in a mesh: dp: 4 (over y, x), chan: 8 (over z, core).
Axes of the slice: x: 2, y: 2, z: 4, core: 2. Of those that a mesh axis runs over, the one named last changes fastest.
Arguments:
- hidden_in: bfloat16 [4096, 8192], P('dp'), may hold values from -6 to 6
- proj_weight: bfloat16 [8192, 4096], P('dp', 'chan'), may hold values from -0.09375 to 0.09375
- embed: bfloat16 [4096, 4096], P('dp', 'chan')
- embed_grad: bfloat16 [4096, 4096], P('dp', 'chan')
- eigvec: float32 [4096, 512], P('chan'), as said below
- eigval: float32 [4096], P('chan'), as said below
Outputs:
- grad_weight: bfloat16 [8192, 4096], P('dp', 'chan')
- grad_hidden: bfloat16 [4096, 8192], P('dp', 'chan')
The draws below stay inside these ranges and needn't reach their ends.
Inputs may be any that keep to these rules, and one draw needn't show every extreme that they name: `eigvec`: each group's block of 512 consecutive rows is an orthogonal matrix whose columns are that group's saved eigenvectors. `eigval`: each group's 512 saved eigenvalues are positive and any two of them differ by at least one percent of the larger.
All inputs are finite; a program needn't handle non-finite values.
Results may differ from the reference program's by a relative error of at most 0.005.
Values may be sent and summed in bfloat16 or wider, within the bound.
A program may use at most 192 MiB of HBM per device.

```python
import math
import jax
import jax.numpy as jnp
from jax import lax

C = 512
DIN = 8192
E = 4096
TOKENS = 4096


def cosine_table(width):
    freq = jnp.arange(width, dtype=jnp.int32)[:, None]
    place = jnp.arange(width, dtype=jnp.int32)[None, :]
    phase = (2 * place + 1) * freq % (4 * width)
    table = math.sqrt(2.0 / width) * jnp.cos(math.pi * phase.astype(jnp.float32) / (2.0 * width))
    first = jnp.where(freq == 0, math.sqrt(0.5), 1.0)
    return (table * first).astype(jnp.float32)


def draw_eigvec(key, part):
    key = jax.random.fold_in(key, 11)
    groups = E // C
    perm_keys = jax.random.split(jax.random.fold_in(key, 1), groups)
    perms = jax.vmap(lambda k: jax.random.permutation(k, C))(perm_keys)
    signs = jax.random.randint(jax.random.fold_in(key, 2), (groups, C), 0, 2) * 2 - 1
    transposed = cosine_table(C).T
    picked = jnp.moveaxis(jnp.take(transposed, perms, axis=1), 1, 0)
    blocks = picked * signs[:, :, None].astype(jnp.float32)
    return blocks.reshape(E, C).astype(jnp.float32)


def draw_eigval(key, part):
    key = jax.random.fold_in(key, 12)
    groups = E // C
    perm_keys = jax.random.split(key, groups)
    perms = jax.vmap(lambda k: jax.random.permutation(k, C))(perm_keys).astype(jnp.float32)
    lowest = 0.1
    spread = 200.0
    values = lowest * jnp.exp(math.log(spread) * perms / (C - 1))
    return values.reshape(E).astype(jnp.float32)


def draw_embed(key, part):
    key = jax.random.fold_in(key, 13)
    place = jnp.arange(TOKENS, dtype=jnp.float32) / (TOKENS - 1)
    offsets = 0.2 * jax.random.truncated_normal(jax.random.fold_in(key, 1), -4.0, 4.0, (E,), jnp.float32)
    noise = jax.random.truncated_normal(jax.random.fold_in(key, 2), -5.0, 5.0, (TOKENS, E), jnp.float32)
    ramp = 1.0 + 2.0 * place
    return (ramp[:, None] * offsets[None, :] + noise).astype(jnp.bfloat16)


def draw_embed_grad(key, part):
    key = jax.random.fold_in(key, 14)
    place = jnp.arange(TOKENS, dtype=jnp.float32) / (TOKENS - 1)
    offsets = 0.2 * jax.random.truncated_normal(jax.random.fold_in(key, 1), -4.0, 4.0, (E,), jnp.float32)
    noise = jax.random.truncated_normal(jax.random.fold_in(key, 2), -5.0, 5.0, (TOKENS, E), jnp.float32)
    ramp = 1.0 + 2.0 * place
    return (ramp[:, None] * offsets[None, :] + noise).astype(jnp.bfloat16)


def raised(drawn, stream_key, source, target, blocks, factor):
    owner, partner = [(jnp.arange(drawn.shape[axis_at]) // (drawn.shape[axis_at] // blocks)).reshape([-1 if axis == axis_at else 1 for axis in range(drawn.ndim)]) for axis_at in (source, target)]
    chosen = jax.random.permutation(stream_key, blocks)[partner]
    strong = (owner == chosen) | (owner == (partner + blocks // 2) % blocks)
    return jnp.where(strong, factor * drawn, drawn)


def level_of(stream_key, extent, cuts, low, top_value):
    loudness = 1.0
    for dim, blocks in cuts:
        steps = jax.random.uniform(jax.random.fold_in(jax.random.fold_in(stream_key, 6), dim), (blocks,), jnp.float32, low / len(cuts), top_value / len(cuts))
        loudness = loudness * jnp.repeat(jnp.exp(steps), extent[dim] // blocks).reshape((-1,) + (1,) * (len(extent) - 1 - dim))
    return loudness


def heavy_noise(own_key, dims, scale, bound, cuts, heavy, kind=jnp.bfloat16):
    drawn = scale * jax.random.normal(own_key, dims, jnp.float32)
    if cuts:
        drawn = drawn * level_of(own_key, dims, cuts, -0.22, 0.18)
    return jnp.clip(raised(drawn, jax.random.fold_in(own_key, 3), *heavy), -bound, bound).astype(kind)


def setup_inputs(seed: int = 0) -> dict:
    key_of = jax.random.split(jax.random.key(seed), 7)
    return {
        "hidden_in": heavy_noise(key_of[0], (TOKENS, DIN), 1.0, 6.0, ((0, 4),), (0, 1, 4, 2.0)),
        "proj_weight": heavy_noise(key_of[1], (DIN, E), DIN ** -0.5, 0.09375, ((0, 4), (1, 8)), (1, 0, 8, 2.0)),
        "embed": draw_embed(jax.random.fold_in(key_of[6], 71), 0),
        "embed_grad": draw_embed_grad(jax.random.fold_in(key_of[6], 71), 0),
        "eigvec": draw_eigvec(jax.random.fold_in(key_of[6], 71), 0),
        "eigval": draw_eigval(jax.random.fold_in(key_of[6], 71), 0),
    }


HI = lax.Precision.HIGHEST

def reference(hidden_in, proj_weight, embed, embed_grad, eigvec, eigval):
    rows = embed.shape[0]
    groups = embed.shape[1] // C
    zfull = embed.astype(jnp.float32)
    gfull = embed_grad.astype(jnp.float32)
    mean_z = lax.optimization_barrier(jnp.sum(zfull, axis=0)) / rows
    mean_g = lax.optimization_barrier(jnp.sum(gfull, axis=0)) / rows
    centered = (zfull - mean_z).reshape(rows, groups, C)
    shifted = (gfull - mean_g).reshape(rows, groups, C)
    grouped = gfull.reshape(rows, groups, C)
    dmat = jnp.einsum('bgc,bgd->gcd', centered, grouped, precision=HI)
    sym = 0.5 * (dmat + jnp.swapaxes(dmat, 1, 2))
    vectors = eigvec.reshape(groups, C, C)
    root = jnp.sqrt(eigval).reshape(groups, C)
    whiten = jnp.einsum('gij,gkj->gik', vectors / root[:, None, :], vectors, precision=HI)
    loewner = -1.0 / (root[:, :, None] * root[:, None, :] * (root[:, :, None] + root[:, None, :]))
    half_rot = jnp.einsum('gji,gjk->gik', vectors, sym, precision=HI)
    rotated = jnp.einsum('gik,gkl->gil', half_rot, vectors, precision=HI)
    inner = loewner * rotated
    half_back = jnp.einsum('gij,gjk->gik', vectors, inner, precision=HI)
    dsigma = jnp.einsum('gik,glk->gil', half_back, vectors, precision=HI)
    first = jnp.einsum('bgc,gcd->bgd', shifted, whiten, precision=HI)
    second = jnp.einsum('bgc,gcd->bgd', centered, dsigma, precision=HI)
    grad_z = (first + 2.0 / rows * second).reshape(rows, groups * C).astype(jnp.bfloat16)
    weight_total = lax.dot_general(hidden_in, grad_z, (((0,), (0,)), ((), ())), preferred_element_type=jnp.float32)
    grad_weight = weight_total.astype(jnp.bfloat16)
    input_total = lax.dot_general(grad_z, proj_weight, (((1,), (1,)), ((), ())), preferred_element_type=jnp.float32)
    grad_hidden = input_total.astype(jnp.bfloat16)
    return (grad_weight, grad_hidden)
```

```python
import jax
import jax.numpy as jnp
from jax import lax
from jax.sharding import PartitionSpec as P

F32, BF16 = jnp.float32, jnp.bfloat16
HI = lax.Precision.HIGHEST
MID = lax.Precision.HIGH


def dot(a, b, dims=((1,), (0,)), precision=None):
    return lax.dot_general(a, b, (dims, ((), ())), precision=precision, preferred_element_type=F32)


def pair(x):
    high = x.astype(BF16)
    return high, (x - high.astype(F32)).astype(BF16)


def local(hidden_in, proj_weight, embed, embed_grad, eigvec, eigval):
    rows = embed.shape[0] * lax.axis_size("dp")
    ones = jnp.ones((8, embed.shape[0]), BF16)
    sums_z, sums_g = dot(ones, embed), dot(ones, embed_grad)
    raw = dot(embed, embed_grad, ((0,), (0,)))
    packed = lax.psum(jnp.concatenate([raw, sums_z, sums_g], axis=0), "dp")
    width = raw.shape[0]
    raw = packed[:width]
    mean_z = packed[width : width + 1] / rows
    mean_g = packed[width + 8 : width + 9] / rows
    dmat = raw - rows * mean_z.T * mean_g
    sym = 0.5 * (dmat + dmat.T)
    root = jnp.sqrt(eigval)
    whiten = dot(eigvec / root[None, :], eigvec, ((1,), (1,)), MID)
    loewner = -1.0 / (root[:, None] * root[None, :] * (root[:, None] + root[None, :]))
    half_rot = dot(eigvec, sym, ((0,), (0,)), MID)
    rotated = dot(half_rot, eigvec, precision=MID)
    half_back = dot(eigvec, loewner * rotated, precision=MID)
    dsigma = dot(half_back, eigvec, ((1,), (1,)), MID) * (2.0 / rows)
    w_hi, w_lo = pair(whiten)
    d_hi, d_lo = pair(dsigma)
    shift = dot(mean_g, whiten, precision=HI) + dot(mean_z, dsigma, precision=HI)
    both = jnp.concatenate([embed_grad, embed], axis=1)
    grad_z = dot(both, jnp.concatenate([w_hi, d_hi], axis=0))
    grad_z += dot(both, jnp.concatenate([w_lo, d_lo], axis=0))
    grad_z = (grad_z - shift).astype(BF16)
    core = lax.rem(lax.axis_index("chan"), 2)
    size = lax.axis_size("chan")
    swap = [(k, k ^ 1) for k in range(size)]
    half = proj_weight.shape[0] // 2
    keep = lax.dynamic_slice_in_dim(proj_weight, core * half, half, 0)
    give = lax.dynamic_slice_in_dim(proj_weight, (1 - core) * half, half, 0)
    mate = lax.ppermute(give, "chan", swap)
    weights = jnp.concatenate([keep, mate], axis=1)
    weights = lax.all_gather(weights, "dp", axis=0, tiled=True)
    both_z = jnp.concatenate([grad_z, lax.ppermute(grad_z, "chan", swap)], axis=1)
    partial_input = dot(both_z, weights, ((1,), (1,))).astype(BF16)
    lines = [list(range(c, size, 2)) for c in range(2)]
    grad_hidden = lax.psum_scatter(
        partial_input, "chan", scatter_dimension=1, axis_index_groups=lines, tiled=True
    )
    partial_weight = dot(hidden_in, grad_z, ((0,), (0,))).astype(BF16)
    grad_weight = lax.psum_scatter(partial_weight, "dp", scatter_dimension=0, tiled=True)
    return (grad_weight, grad_hidden)


def solution(mesh):
    in_specs = (
        P("dp", None),
        P("dp", "chan"),
        P("dp", "chan"),
        P("dp", "chan"),
        P("chan", None),
        P("chan"),
    )
    out_specs = (P("dp", "chan"), P("dp", "chan"))
    return jax.shard_map(local, mesh=mesh, in_specs=in_specs, out_specs=out_specs, check_vma=False)
```

```python
import jax
import jax.numpy as jnp
from jax import lax
from jax.experimental import pallas as pl
from jax.experimental.pallas import tpu as pltpu
from jax.sharding import PartitionSpec as P

F32, BF16 = jnp.float32, jnp.bfloat16
HI = lax.Precision.HIGHEST
MID = lax.Precision.HIGH
MESH = pl.DeviceIdType.MESH


def dot(a, b, dims=((1,), (0,)), precision=None):
    return lax.dot_general(a, b, (dims, ((), ())), precision=precision, preferred_element_type=F32)


def pair(x):
    high = x.astype(BF16)
    return high, (x - high.astype(F32)).astype(BF16)


def local(hidden_in, proj_weight, embed, embed_grad, eigvec, eigval):
    rows = embed.shape[0] * lax.axis_size("dp")
    ones = jnp.ones((8, embed.shape[0]), BF16)
    sums_z, sums_g = dot(ones, embed), dot(ones, embed_grad)
    raw = dot(embed, embed_grad, ((0,), (0,)))
    packed = lax.psum(jnp.concatenate([raw, sums_z, sums_g], axis=0), "dp")
    width = raw.shape[0]
    raw = packed[:width]
    mean_z = packed[width : width + 1] / rows
    mean_g = packed[width + 8 : width + 9] / rows
    dmat = raw - rows * mean_z.T * mean_g
    sym = 0.5 * (dmat + dmat.T)
    root = jnp.sqrt(eigval)
    whiten = dot(eigvec / root[None, :], eigvec, ((1,), (1,)), MID)
    loewner = -1.0 / (root[:, None] * root[None, :] * (root[:, None] + root[None, :]))
    half_rot = dot(eigvec, sym, ((0,), (0,)), MID)
    rotated = dot(half_rot, eigvec, precision=MID)
    half_back = dot(eigvec, loewner * rotated, precision=MID)
    dsigma = dot(half_back, eigvec, ((1,), (1,)), MID) * (2.0 / rows)
    w_hi, w_lo = pair(whiten)
    d_hi, d_lo = pair(dsigma)
    shift = dot(mean_g, whiten, precision=HI) + dot(mean_z, dsigma, precision=HI)
    both = jnp.concatenate([embed_grad, embed], axis=1)
    grad_z = dot(both, jnp.concatenate([w_hi, d_hi], axis=0))
    grad_z += dot(both, jnp.concatenate([w_lo, d_lo], axis=0))
    grad_z = (grad_z - shift).astype(BF16)
    core = lax.rem(lax.axis_index("chan"), 2)
    size = lax.axis_size("chan")
    swap = [(k, k ^ 1) for k in range(size)]
    half = proj_weight.shape[0] // 2
    keep = lax.dynamic_slice_in_dim(proj_weight, core * half, half, 0)
    give = lax.dynamic_slice_in_dim(proj_weight, (1 - core) * half, half, 0)
    mate = lax.ppermute(give, "chan", swap)
    weights = jnp.concatenate([keep, mate], axis=1)
    weights = lax.all_gather(weights, "dp", axis=0, tiled=True)
    both_z = jnp.concatenate([grad_z, lax.ppermute(grad_z, "chan", swap)], axis=1)
    partial_input = dot(both_z, weights, ((1,), (1,))).astype(BF16)
    lines = [list(range(c, size, 2)) for c in range(2)]
    grad_hidden = lax.psum_scatter(
        partial_input, "chan", scatter_dimension=1, axis_index_groups=lines, tiled=True
    )
    partial_weight = dot(hidden_in, grad_z, ((0,), (0,))).astype(BF16)
    grad_weight = lax.psum_scatter(partial_weight, "dp", scatter_dimension=0, tiled=True)
    return (grad_weight, grad_hidden)


def dot3(a, b):
    a_hi, a_lo = pair(a)
    b_hi, b_lo = pair(b)
    return dot(a_hi, b_hi) + (dot(a_hi, b_lo) + dot(a_lo, b_hi))


def fused(
    hid, w4, z_ref, g_ref, u_ref, ev_ref, gw_ref, gh_ref,
    mom, mom_in, sums, dmat, mats, shift, gz, gzt, wsc, wf, hb,
    a1s, a1r, a2s, a2r, b1s, b1r, b2s, b2r,
    mom_ss, mom_rs, sum_ss, sum_rs, dm_ss, dm_rs, w1_ss, w1_rs, w2_ss, w2_rs, wg_ss, wg_rs,
    rt_ss, rt_rs, lt_ss, lt_rs, sr_ss, sr_rs, sl_ss, sl_rs, red_ss, red_rs, loc,
):
    dp, chan = lax.axis_index("dp"), lax.axis_index("chan")
    px, py = lax.rem(dp, 2), dp // 2
    xn, yn, dg = 2 * py + (1 - px), 2 * (1 - py) + px, 2 * (1 - py) + (1 - px)
    zc, core = chan // 2, lax.rem(chan, 2)
    mate = 2 * zc + (1 - core)
    tokens, width = z_ref.shape
    rows = 4 * tokens
    quarter = width // 4
    part = wf.shape[1] // 4
    half = hb.shape[2]
    last = 3

    def plane(d):
        return lax.rem(dp + d, 4)

    def line(d):
        return lax.rem(chan + d, 8)

    def rdma(src, dst, ss, rs, where):
        return pltpu.make_async_remote_copy(
            src_ref=src, dst_ref=dst, send_sem=ss, recv_sem=rs, device_id=where, device_id_type=MESH
        )

    barrier = pltpu.get_barrier_semaphore()
    for d in range(1, 4):
        pl.semaphore_signal(barrier, inc=1, device_id={"dp": plane(d)}, device_id_type=MESH)
    for d in range(1, 8):
        pl.semaphore_signal(barrier, inc=1, device_id={"chan": line(d)}, device_id_type=MESH)

    order = [(dg, 0), (dg, 1), (xn, 0), (yn, 1), (yn, 0), (xn, 1), (dp, 0), (dp, 1)]
    slots = hb.shape[0]

    def fetch(n):
        block, side = order[n]
        start = pl.multiple_of(block * (2 * half) + side * half, half)
        return pltpu.make_async_copy(hid.at[:, pl.ds(start, half)], hb.at[n % slots], loc.at[n % slots])

    for n in range(slots):
        fetch(n).start()

    ones = jnp.ones((8, tokens), BF16)
    sums[dp, 0:8, :] = dot(ones, z_ref[...])
    sums[dp, 8:16, :] = dot(ones, g_ref[...])
    z_t = z_ref[...].astype(F32).T.astype(BF16)
    mom[...] = dot(z_t, g_ref[...])

    pl.semaphore_wait(barrier, 10)
    sends = []

    def go(copy):
        copy.start()
        sends.append(copy)
        return copy

    mom_c, sum_c, w1_c = [], [], []
    for d in range(1, 4):
        to = plane(d)
        where = {"dp": to}
        start = pl.multiple_of(to * quarter, quarter)
        mom_c.append(go(rdma(mom.at[pl.ds(start, quarter)], mom_in.at[d], mom_ss.at[d], mom_rs.at[d], where)))
        sum_c.append(go(rdma(sums.at[dp], sums.at[dp], sum_ss.at[d], sum_rs.at[d], where)))
    for d in range(1, 4):
        to = plane(d)
        w1_c.append(go(rdma(w4.at[:, to], wsc.at[dp], w1_ss.at[d], w1_rs.at[d], {"dp": to})))
    own_w = pltpu.make_async_copy(w4.at[:, dp], wsc.at[dp], loc.at[slots])
    own_w.start()

    u = u_ref[...]
    root_row = jnp.broadcast_to(jnp.sqrt(ev_ref[...]), (width, width))
    u_t = u.T
    whiten = dot3(u / root_row, u_t)
    mats[0], mats[1] = pair(whiten)
    root_col = root_row.T
    loewner = -1.0 / (root_row * root_col * (root_row + root_col))

    for c in mom_c:
        c.wait_recv()
    mine = pl.ds(pl.multiple_of(dp * quarter, quarter), quarter)
    dmat[mine, :] = (mom[mine, :] + mom_in[1]) + (mom_in[2] + mom_in[3])
    dm_c = []
    for d in range(1, 4):
        dm_c.append(go(rdma(dmat.at[mine], dmat.at[mine], dm_ss.at[d], dm_rs.at[d], {"dp": plane(d)})))
    for c in sum_c:
        c.wait_recv()
    for c in w1_c:
        c.wait_recv()
    own_w.wait()
    my_part = pl.ds(pl.multiple_of(dp * part, part), part)
    w2_c = []
    for d in range(1, 8):
        to = line(d)
        w2_c.append(
            go(
                rdma(
                    wsc.at[to // 2, lax.rem(to, 2)], wf.at[chan, my_part],
                    w2_ss.at[d], w2_rs.at[d], {"chan": to},
                )
            )
        )
    own_w2 = pltpu.make_async_copy(wsc.at[zc, core], wf.at[chan, my_part], loc.at[slots])
    own_w2.start()
    for c in dm_c:
        c.wait_recv()

    total = (sums[0] + sums[1]) + (sums[2] + sums[3])
    mean_z, mean_g = total[0:8] / rows, total[8:16] / rows
    col_z = jnp.broadcast_to(mean_z[0:1], (width, width)).T
    raw = dmat[...] - rows * col_z * mean_g[0:1]
    sym = 0.5 * (raw + raw.T)
    rotated = dot3(dot3(u_t, sym), u)
    dsigma = dot3(dot3(u, loewner * rotated), u_t) * (2.0 / rows)
    mats[2], mats[3] = pair(dsigma)
    shift[...] = dot3(mean_g, whiten) + dot3(mean_z, dsigma)

    tile = tokens // 4

    @pl.loop(0, 4)
    def _(t):
        here = pl.ds(pl.multiple_of(t * tile, tile), tile)
        g, z = g_ref[here, :], z_ref[here, :]
        acc = (dot(g, mats[0]) + dot(z, mats[2])) + (dot(g, mats[1]) + dot(z, mats[3]))
        acc = acc - shift[0:1, :]
        gz[chan, here, :] = acc.astype(BF16)
        gzt[:, here] = acc.T.astype(BF16)

    def moves_right(k):
        slot = 2 * (zc - k) + core
        return rdma(gz.at[slot], gz.at[slot], rt_ss.at[k], rt_rs.at[k], {"chan": chan + 2})

    def moves_left(k):
        slot = 2 * (zc + k) + core
        return rdma(gz.at[slot], gz.at[slot], lt_ss.at[k], lt_rs.at[k], {"chan": chan - 2})

    def from_left(k):
        slot = 2 * (zc - 1 - k) + core
        return rdma(gz.at[slot], gz.at[slot], rt_ss.at[k], rt_rs.at[k], {"chan": chan - 2})

    def from_right(k):
        slot = 2 * (zc + 1 + k) + core
        return rdma(gz.at[slot], gz.at[slot], lt_ss.at[k], lt_rs.at[k], {"chan": chan + 2})

    def to_mate(block, ss, rs):
        slot = 2 * block + core
        return rdma(gz.at[slot], gz.at[slot], ss, rs, {"chan": mate})

    def has_left(k):
        return zc - 1 - k >= 0

    def has_right(k):
        return zc + 1 + k <= last

    def sends_right(k):
        return jnp.logical_and(zc - k >= 0, zc < last)

    def sends_left(k):
        return jnp.logical_and(zc + k <= last, zc > 0)

    def push(k):
        pl.when(sends_right(k))(lambda: moves_right(k).start())
        pl.when(sends_left(k))(lambda: moves_left(k).start())

    def take(k):
        @pl.when(has_left(k))
        def _():
            from_left(k).wait_recv()
            if k < 2:
                pl.when(zc < last)(lambda: moves_right(k + 1).start())
            to_mate(zc - 1 - k, sr_ss.at[k], sr_rs.at[k]).start()

        @pl.when(has_right(k))
        def _():
            from_right(k).wait_recv()
            if k < 2:
                pl.when(zc > 0)(lambda: moves_left(k + 1).start())
            to_mate(zc + 1 + k, sl_ss.at[k], sl_rs.at[k]).start()

    push(0)
    own_mate = go(to_mate(zc, sr_ss.at[3], sr_rs.at[3]))

    cols = half // 4

    def product(n, emit):
        fetch(n).wait()

        @pl.loop(0, 4)
        def _(t):
            here = pl.ds(pl.multiple_of(t * cols, cols), cols)
            emit(here, dot(gzt[...], hb[n % slots, :, here]))

        if n + slots < len(order):
            fetch(n + slots).start()

    def store(dst, idx):
        def emit(here, value):
            dst[idx, :, here] = value.astype(BF16)

        return emit

    to_x, to_y = {"dp": xn}, {"dp": yn}
    product(0, store(a1s, 1))
    a1_dg = go(rdma(a1s.at[1], a1r.at[1], red_ss.at[0], red_rs.at[0], to_x))
    product(1, store(b1s, 1))
    b1_dg = go(rdma(b1s.at[1], b1r.at[1], red_ss.at[1], red_rs.at[1], to_y))
    product(2, store(a1s, 0))
    a1_own = go(rdma(a1s.at[0], a1r.at[0], red_ss.at[2], red_rs.at[2], to_x))
    product(3, store(b1s, 0))
    b1_own = go(rdma(b1s.at[0], b1r.at[0], red_ss.at[3], red_rs.at[3], to_y))

    take(0)
    for c in w2_c:
        c.wait_recv()
    own_w2.wait()
    wg_x = go(rdma(wf.at[:, my_part], wf.at[:, my_part], wg_ss.at[0], wg_rs.at[0], to_x))
    wg_y = go(rdma(wf.at[:, my_part], wf.at[:, my_part], wg_ss.at[1], wg_rs.at[1], to_y))

    def store_sum(dst, more):
        def emit(here, value):
            dst[:, here] = (value + more[1, :, here].astype(F32)).astype(BF16)

        return emit

    a1_dg.wait_recv()
    product(4, store_sum(a2s, a1r))
    a2 = go(rdma(a2s, a2r, red_ss.at[4], red_rs.at[4], to_y))
    b1_dg.wait_recv()
    product(5, store_sum(b2s, b1r))
    b2 = go(rdma(b2s, b2r, red_ss.at[5], red_rs.at[5], to_x))

    take(1)
    half_part = part // 2
    wg_y.wait_recv()
    first = pl.ds(pl.multiple_of(yn * part, part), half_part)
    relay_x = go(rdma(wf.at[:, first], wf.at[:, first], wg_ss.at[2], wg_rs.at[2], to_x))
    wg_x.wait_recv()
    second = pl.ds(pl.multiple_of(xn * part + half_part, half_part), half_part)
    relay_y = go(rdma(wf.at[:, second], wf.at[:, second], wg_ss.at[3], wg_rs.at[3], to_y))
    take(2)

    own_mate.wait_recv()
    for k in range(3):
        pl.when(has_left(k))(lambda k=k: to_mate(zc - 1 - k, sr_ss.at[k], sr_rs.at[k]).wait_recv())
        pl.when(has_right(k))(lambda k=k: to_mate(zc + 1 + k, sl_ss.at[k], sl_rs.at[k]).wait_recv())

    def hidden_part(owner):
        these = pl.ds(pl.multiple_of(owner * part, part), part)
        block = tokens // 2

        @pl.loop(0, 2)
        def _(t):
            here = pl.ds(pl.multiple_of(t * block, block), block)
            acc = dot(gz[0, here, :], wf[0, these, :], ((1,), (1,)))
            for e in range(1, 8):
                acc += dot(gz[e, here, :], wf[e, these, :], ((1,), (1,)))
            gh_ref[here, these] = acc.astype(BF16)

    hidden_part(dp)
    hidden_part(xn)
    hidden_part(yn)

    def finish(side, first_in, second_in):
        def emit(here, value):
            value = value + first_in[0, :, here].astype(F32) + second_in[:, here].astype(F32)
            to = pl.ds(pl.multiple_of(side * half + here.start, cols), cols)
            gw_ref[to, :] = value.T.astype(BF16)

        return emit

    a1_own.wait_recv()
    a2.wait_recv()
    product(6, finish(0, a1r, a2r))
    b1_own.wait_recv()
    b2.wait_recv()
    product(7, finish(1, b1r, b2r))
    relay_x.wait_recv()
    relay_y.wait_recv()
    hidden_part(dg)

    for c in sends:
        c.wait_send()
    for k in range(3):
        pl.when(sends_right(k))(lambda k=k: moves_right(k).wait_send())
        pl.when(sends_left(k))(lambda k=k: moves_left(k).wait_send())
        pl.when(has_left(k))(lambda k=k: to_mate(zc - 1 - k, sr_ss.at[k], sr_rs.at[k]).wait_send())
        pl.when(has_right(k))(lambda k=k: to_mate(zc + 1 + k, sl_ss.at[k], sl_rs.at[k]).wait_send())


def local_fused(hidden_in, proj_weight, embed, embed_grad, eigvec, eigval):
    tokens, width = embed.shape
    feats = proj_weight.shape[0]
    part, half = feats // 8, feats // 2
    vmem, anyspace = pl.BlockSpec(memory_space=pltpu.VMEM), pl.BlockSpec(memory_space=pl.ANY)
    dma = pltpu.SemaphoreType.DMA
    slots = 4
    return pl.pallas_call(
        fused,
        out_shape=(
            jax.ShapeDtypeStruct((feats, width), BF16),
            jax.ShapeDtypeStruct((tokens, half), BF16),
        ),
        in_specs=[anyspace, anyspace, vmem, vmem, vmem, vmem],
        out_specs=(vmem, vmem),
        scratch_shapes=[
            pltpu.VMEM((width, width), F32),
            pltpu.VMEM((4, width // 4, width), F32),
            pltpu.VMEM((4, 16, width), F32),
            pltpu.VMEM((width, width), F32),
            pltpu.VMEM((4, width, width), BF16),
            pltpu.VMEM((8, width), F32),
            pltpu.VMEM((8, tokens, width), BF16),
            pltpu.VMEM((width, tokens), BF16),
            pltpu.VMEM((4, 2, part, width), BF16),
            pltpu.VMEM((8, half, width), BF16),
            pltpu.VMEM((slots, tokens, half), BF16),
        ]
        + [
            pltpu.VMEM((2, width, half), BF16),
            pltpu.VMEM((2, width, half), BF16),
            pltpu.VMEM((width, half), BF16),
            pltpu.VMEM((width, half), BF16),
        ]
        * 2
        + [dma((4,))] * 8
        + [dma((8,))] * 2
        + [dma((4,))] * 10
        + [dma((6,))] * 2
        + [dma((slots + 1,))],
        compiler_params=pltpu.CompilerParams(
            collective_id=0, has_side_effects=True, vmem_limit_bytes=63 * 2**20
        ),
        cost_estimate=pl.CostEstimate(flops=20 * 10**9, bytes_accessed=30 * 10**6, transcendentals=0),
    )(
        hidden_in,
        proj_weight.reshape(2, 4, part, width),
        embed,
        embed_grad,
        eigvec,
        eigval.reshape(1, width),
    )


def solution(mesh):
    in_specs = (
        P("dp", None),
        P("dp", "chan"),
        P("dp", "chan"),
        P("dp", "chan"),
        P("chan", None),
        P("chan"),
    )
    out_specs = (P("dp", "chan"), P("dp", "chan"))
    small = mesh.shape["dp"] == 4 and mesh.shape["chan"] == 8
    run = local_fused if small else local
    return jax.shard_map(run, mesh=mesh, in_specs=in_specs, out_specs=out_specs, check_vma=False)
```

```python
import jax
import jax.numpy as jnp
from jax import lax
from jax.experimental import pallas as pl
from jax.experimental.pallas import tpu as pltpu
from jax.sharding import PartitionSpec as P

F32, BF16 = jnp.float32, jnp.bfloat16
HI = lax.Precision.HIGHEST
MID = lax.Precision.HIGH
MESH = pl.DeviceIdType.MESH


def dot(a, b, dims=((1,), (0,)), precision=None):
    return lax.dot_general(a, b, (dims, ((), ())), precision=precision, preferred_element_type=F32)


def pair(x):
    high = x.astype(BF16)
    return high, (x - high.astype(F32)).astype(BF16)


def local(hidden_in, proj_weight, embed, embed_grad, eigvec, eigval):
    rows = embed.shape[0] * lax.axis_size("dp")
    ones = jnp.ones((8, embed.shape[0]), BF16)
    sums_z, sums_g = dot(ones, embed), dot(ones, embed_grad)
    raw = dot(embed, embed_grad, ((0,), (0,)))
    packed = lax.psum(jnp.concatenate([raw, sums_z, sums_g], axis=0), "dp")
    width = raw.shape[0]
    raw = packed[:width]
    mean_z = packed[width : width + 1] / rows
    mean_g = packed[width + 8 : width + 9] / rows
    dmat = raw - rows * mean_z.T * mean_g
    sym = 0.5 * (dmat + dmat.T)
    root = jnp.sqrt(eigval)
    whiten = dot(eigvec / root[None, :], eigvec, ((1,), (1,)), MID)
    loewner = -1.0 / (root[:, None] * root[None, :] * (root[:, None] + root[None, :]))
    half_rot = dot(eigvec, sym, ((0,), (0,)), MID)
    rotated = dot(half_rot, eigvec, precision=MID)
    half_back = dot(eigvec, loewner * rotated, precision=MID)
    dsigma = dot(half_back, eigvec, ((1,), (1,)), MID) * (2.0 / rows)
    w_hi, w_lo = pair(whiten)
    d_hi, d_lo = pair(dsigma)
    shift = dot(mean_g, whiten, precision=HI) + dot(mean_z, dsigma, precision=HI)
    both = jnp.concatenate([embed_grad, embed], axis=1)
    grad_z = dot(both, jnp.concatenate([w_hi, d_hi], axis=0))
    grad_z += dot(both, jnp.concatenate([w_lo, d_lo], axis=0))
    grad_z = (grad_z - shift).astype(BF16)
    core = lax.rem(lax.axis_index("chan"), 2)
    size = lax.axis_size("chan")
    swap = [(k, k ^ 1) for k in range(size)]
    half = proj_weight.shape[0] // 2
    keep = lax.dynamic_slice_in_dim(proj_weight, core * half, half, 0)
    give = lax.dynamic_slice_in_dim(proj_weight, (1 - core) * half, half, 0)
    mate = lax.ppermute(give, "chan", swap)
    weights = jnp.concatenate([keep, mate], axis=1)
    weights = lax.all_gather(weights, "dp", axis=0, tiled=True)
    both_z = jnp.concatenate([grad_z, lax.ppermute(grad_z, "chan", swap)], axis=1)
    partial_input = dot(both_z, weights, ((1,), (1,))).astype(BF16)
    lines = [list(range(c, size, 2)) for c in range(2)]
    grad_hidden = lax.psum_scatter(
        partial_input, "chan", scatter_dimension=1, axis_index_groups=lines, tiled=True
    )
    partial_weight = dot(hidden_in, grad_z, ((0,), (0,))).astype(BF16)
    grad_weight = lax.psum_scatter(partial_weight, "dp", scatter_dimension=0, tiled=True)
    return (grad_weight, grad_hidden)


def dot3(a, b):
    a_hi, a_lo = pair(a)
    b_hi, b_lo = pair(b)
    return dot(a_hi, b_hi) + (dot(a_hi, b_lo) + dot(a_lo, b_hi))


def fused(
    hid, w4, z_ref, g_ref, u_ref, ev_ref, gw_ref, gh_ref,
    mom, mom_in, sums, dmat, mats, shift, acc_t, gz, gzt, wsc, wf, hb,
    a1s, a1r, a2s, a2r, b1s, b1r, b2s, b2r,
    mom_ss, mom_rs, sum_ss, sum_rs, dm_ss, dm_rs, w1_ss, w1_rs, w2_ss, w2_rs, wg_ss, wg_rs,
    rt_ss, rt_rs, lt_ss, lt_rs, sr_ss, sr_rs, sl_ss, sl_rs, red_ss, red_rs, loc,
):
    dp, chan = lax.axis_index("dp"), lax.axis_index("chan")
    px, py = lax.rem(dp, 2), dp // 2
    xn, yn, dg = 2 * py + (1 - px), 2 * (1 - py) + px, 2 * (1 - py) + (1 - px)
    zc, core = chan // 2, lax.rem(chan, 2)
    mate = 2 * zc + (1 - core)
    tokens, width = z_ref.shape
    rows = 4 * tokens
    quarter = width // 4
    part = wf.shape[1] // 4
    half = hb.shape[2]
    last = 3

    def plane(d):
        return lax.rem(dp + d, 4)

    def line(d):
        return lax.rem(chan + d, 8)

    def rdma(src, dst, ss, rs, where):
        return pltpu.make_async_remote_copy(
            src_ref=src, dst_ref=dst, send_sem=ss, recv_sem=rs, device_id=where, device_id_type=MESH
        )

    barrier = pltpu.get_barrier_semaphore()
    for d in range(1, 4):
        pl.semaphore_signal(barrier, inc=1, device_id={"dp": plane(d)}, device_id_type=MESH)
    for d in range(1, 8):
        pl.semaphore_signal(barrier, inc=1, device_id={"chan": line(d)}, device_id_type=MESH)

    order = [(dg, 0), (dg, 1), (xn, 0), (yn, 1), (yn, 0), (xn, 1), (dp, 0), (dp, 1)]
    slots = hb.shape[0]

    def fetch(n):
        block, side = order[n]
        start = pl.multiple_of(block * (2 * half) + side * half, half)
        return pltpu.make_async_copy(hid.at[:, pl.ds(start, half)], hb.at[n % slots], loc.at[n % slots])

    for n in range(slots):
        fetch(n).start()

    ones = jnp.ones((8, tokens), BF16)
    sums[dp, 0:8, :] = dot(ones, z_ref[...])
    sums[dp, 8:16, :] = dot(ones, g_ref[...])
    z_t = z_ref[...].astype(F32).T.astype(BF16)
    mom[...] = dot(z_t, g_ref[...])

    pl.semaphore_wait(barrier, 10)
    sends = []

    def go(copy):
        copy.start()
        sends.append(copy)
        return copy

    mom_c, sum_c, w1_c = [], [], []
    for d in range(1, 4):
        to = plane(d)
        where = {"dp": to}
        start = pl.multiple_of(to * quarter, quarter)
        mom_c.append(go(rdma(mom.at[pl.ds(start, quarter)], mom_in.at[d], mom_ss.at[d], mom_rs.at[d], where)))
        sum_c.append(go(rdma(sums.at[dp], sums.at[dp], sum_ss.at[d], sum_rs.at[d], where)))
    for d in range(1, 4):
        to = plane(d)
        w1_c.append(go(rdma(w4.at[:, to], wsc.at[dp], w1_ss.at[d], w1_rs.at[d], {"dp": to})))
    own_w = pltpu.make_async_copy(w4.at[:, dp], wsc.at[dp], loc.at[slots])
    own_w.start()

    u = u_ref[...]
    root_row = jnp.broadcast_to(jnp.sqrt(ev_ref[...]), (width, width))
    u_t = u.T
    whiten = dot3(u / root_row, u_t)
    mats[0], mats[1] = pair(whiten)
    root_col = root_row.T
    loewner = -1.0 / (root_row * root_col * (root_row + root_col))

    for c in mom_c:
        c.wait_recv()
    mine = pl.ds(pl.multiple_of(dp * quarter, quarter), quarter)
    dmat[mine, :] = (mom[mine, :] + mom_in[1]) + (mom_in[2] + mom_in[3])
    dm_c = []
    for d in range(1, 4):
        dm_c.append(go(rdma(dmat.at[mine], dmat.at[mine], dm_ss.at[d], dm_rs.at[d], {"dp": plane(d)})))
    for c in sum_c:
        c.wait_recv()
    for c in w1_c:
        c.wait_recv()
    own_w.wait()
    my_part = pl.ds(pl.multiple_of(dp * part, part), part)
    w2_c = []
    for d in range(1, 8):
        to = line(d)
        w2_c.append(
            go(
                rdma(
                    wsc.at[to // 2, lax.rem(to, 2)], wf.at[chan, my_part],
                    w2_ss.at[d], w2_rs.at[chan], {"chan": to},
                )
            )
        )
    own_w2 = pltpu.make_async_copy(wsc.at[zc, core], wf.at[chan, my_part], loc.at[slots])
    own_w2.start()

    to_x, to_y = {"dp": xn}, {"dp": yn}
    half_part = part // 2

    def landed(source):
        ref = wf.at[source, my_part]
        rdma(ref, ref, w2_ss.at[0], w2_rs.at[source], {"chan": mate}).wait_recv()

    def group(k):
        return pl.ds(2 * lax.rem(zc + k, 4), 2)

    def spread(k):
        ref = wf.at[group(k), my_part]
        wg_c.append(
            [
                go(rdma(ref, ref, wg_ss.at[4 * n + k], wg_rs.at[4 * n + k], where))
                for n, where in enumerate((to_x, to_y))
            ]
        )

    def relay(k):
        ways = (
            (2, wg_c[k][1], yn * part, to_x),
            (3, wg_c[k][0], xn * part + half_part, to_y),
        )
        for n, arrived, start, where in ways:
            arrived.wait_recv()
            ref = wf.at[group(k), pl.ds(pl.multiple_of(start, half_part), half_part)]
            relay_c.append(go(rdma(ref, ref, wg_ss.at[4 * n + k], wg_rs.at[4 * n + k], where)))

    wg_c, relay_c = [], []
    own_w2.wait()
    landed(mate)
    spread(0)
    for c in dm_c:
        c.wait_recv()

    total = (sums[0] + sums[1]) + (sums[2] + sums[3])
    mean_z, mean_g = total[0:8] / rows, total[8:16] / rows
    col_z = jnp.broadcast_to(mean_z[0:1], (width, width)).T
    raw = dmat[...] - rows * col_z * mean_g[0:1]
    sym = 0.5 * (raw + raw.T)
    rotated = dot3(dot3(u_t, sym), u)
    dsigma = dot3(dot3(u, loewner * rotated), u_t) * (2.0 / rows)
    mats[2], mats[3] = pair(dsigma)
    shift[...] = dot3(mean_g, whiten) + dot3(mean_z, dsigma)

    tile = tokens // 4

    @pl.loop(0, 4)
    def _(t):
        here = pl.ds(pl.multiple_of(t * tile, tile), tile)
        g, z = g_ref[here, :], z_ref[here, :]
        acc = (dot(g, mats[0]) + dot(z, mats[2])) + (dot(g, mats[1]) + dot(z, mats[3]))
        acc = acc - shift[0:1, :]
        gz[chan, here, :] = acc.astype(BF16)
        gzt[:, here] = acc.T.astype(BF16)

    def moves_right(k):
        slot = 2 * (zc - k) + core
        return rdma(gz.at[slot], gz.at[slot], rt_ss.at[k], rt_rs.at[k], {"chan": chan + 2})

    def moves_left(k):
        slot = 2 * (zc + k) + core
        return rdma(gz.at[slot], gz.at[slot], lt_ss.at[k], lt_rs.at[k], {"chan": chan - 2})

    def from_left(k):
        slot = 2 * (zc - 1 - k) + core
        return rdma(gz.at[slot], gz.at[slot], rt_ss.at[k], rt_rs.at[k], {"chan": chan - 2})

    def from_right(k):
        slot = 2 * (zc + 1 + k) + core
        return rdma(gz.at[slot], gz.at[slot], lt_ss.at[k], lt_rs.at[k], {"chan": chan + 2})

    def to_mate(block, ss, rs):
        slot = 2 * block + core
        return rdma(gz.at[slot], gz.at[slot], ss, rs, {"chan": mate})

    def has_left(k):
        return zc - 1 - k >= 0

    def has_right(k):
        return zc + 1 + k <= last

    def sends_right(k):
        return jnp.logical_and(zc - k >= 0, zc < last)

    def sends_left(k):
        return jnp.logical_and(zc + k <= last, zc > 0)

    def push(k):
        pl.when(sends_right(k))(lambda: moves_right(k).start())
        pl.when(sends_left(k))(lambda: moves_left(k).start())

    def take(k):
        @pl.when(has_left(k))
        def _():
            from_left(k).wait_recv()
            if k < 2:
                pl.when(zc < last)(lambda: moves_right(k + 1).start())
            to_mate(zc - 1 - k, sr_ss.at[k], sr_rs.at[k]).start()

        @pl.when(has_right(k))
        def _():
            from_right(k).wait_recv()
            if k < 2:
                pl.when(zc > 0)(lambda: moves_left(k + 1).start())
            to_mate(zc + 1 + k, sl_ss.at[k], sl_rs.at[k]).start()

    push(0)
    own_mate = go(to_mate(zc, sr_ss.at[3], sr_rs.at[3]))

    cols = half // 4

    def product(n, emit):
        fetch(n).wait()

        @pl.loop(0, 4)
        def _(t):
            here = pl.ds(pl.multiple_of(t * cols, cols), cols)
            emit(here, dot(gzt[...], hb[n % slots, :, here]))

        if n + slots < len(order):
            fetch(n + slots).start()

    def store(dst, idx):
        def emit(here, value):
            dst[idx, :, here] = value.astype(BF16)

        return emit

    product(0, store(a1s, 1))
    a1_dg = go(rdma(a1s.at[1], a1r.at[1], red_ss.at[0], red_rs.at[0], to_x))
    product(1, store(b1s, 1))
    b1_dg = go(rdma(b1s.at[1], b1r.at[1], red_ss.at[1], red_rs.at[1], to_y))

    def next_group(k):
        for c in range(2):
            landed(2 * lax.rem(zc + k, 4) + c)
        spread(k)

    next_group(1)
    relay(0)
    product(2, store(a1s, 0))
    a1_own = go(rdma(a1s.at[0], a1r.at[0], red_ss.at[2], red_rs.at[2], to_x))
    product(3, store(b1s, 0))
    b1_own = go(rdma(b1s.at[0], b1r.at[0], red_ss.at[3], red_rs.at[3], to_y))
    take(0)
    next_group(2)
    next_group(3)

    def store_sum(dst, more):
        def emit(here, value):
            dst[:, here] = (value + more[1, :, here].astype(F32)).astype(BF16)

        return emit

    a1_dg.wait_recv()
    product(4, store_sum(a2s, a1r))
    a2 = go(rdma(a2s, a2r, red_ss.at[4], red_rs.at[4], to_y))
    b1_dg.wait_recv()
    product(5, store_sum(b2s, b1r))
    b2 = go(rdma(b2s, b2r, red_ss.at[5], red_rs.at[5], to_x))
    relay(1)
    take(1)

    def keep(side, first_in):
        def emit(here, value):
            acc_t[side, :, here] = value + first_in[0, :, here].astype(F32)

        return emit

    relay(2)
    a1_own.wait_recv()
    product(6, keep(0, a1r))
    b1_own.wait_recv()
    product(7, keep(1, b1r))
    relay(3)
    take(2)

    own_mate.wait_recv()
    for k in range(3):
        pl.when(has_left(k))(lambda k=k: to_mate(zc - 1 - k, sr_ss.at[k], sr_rs.at[k]).wait_recv())
        pl.when(has_right(k))(lambda k=k: to_mate(zc + 1 + k, sl_ss.at[k], sl_rs.at[k]).wait_recv())

    def hidden_part(owner):
        these = pl.ds(pl.multiple_of(owner * part, part), part)
        block = tokens // 2

        @pl.loop(0, 2)
        def _(t):
            here = pl.ds(pl.multiple_of(t * block, block), block)
            acc = dot(gz[0, here, :], wf[0, these, :], ((1,), (1,)))
            for e in range(1, 8):
                acc += dot(gz[e, here, :], wf[e, these, :], ((1,), (1,)))
            gh_ref[here, these] = acc.astype(BF16)

    hidden_part(dp)
    hidden_part(xn)
    hidden_part(yn)

    for side, arrived, ref in ((0, a2, a2r), (1, b2, b2r)):
        arrived.wait_recv()

        @pl.loop(0, 4)
        def _(t):
            start = pl.multiple_of(t * cols, cols)
            here = pl.ds(start, cols)
            value = acc_t[side, :, here] + ref[:, here].astype(F32)
            gw_ref[pl.ds(pl.multiple_of(side * half + start, cols), cols), :] = value.T.astype(BF16)

    for c in relay_c:
        c.wait_recv()
    hidden_part(dg)

    for c in sends:
        c.wait_send()
    for k in range(3):
        pl.when(sends_right(k))(lambda k=k: moves_right(k).wait_send())
        pl.when(sends_left(k))(lambda k=k: moves_left(k).wait_send())
        pl.when(has_left(k))(lambda k=k: to_mate(zc - 1 - k, sr_ss.at[k], sr_rs.at[k]).wait_send())
        pl.when(has_right(k))(lambda k=k: to_mate(zc + 1 + k, sl_ss.at[k], sl_rs.at[k]).wait_send())


def local_fused(hidden_in, proj_weight, embed, embed_grad, eigvec, eigval):
    tokens, width = embed.shape
    feats = proj_weight.shape[0]
    part, half = feats // 8, feats // 2
    vmem, anyspace = pl.BlockSpec(memory_space=pltpu.VMEM), pl.BlockSpec(memory_space=pl.ANY)
    dma = pltpu.SemaphoreType.DMA
    slots = 4
    return pl.pallas_call(
        fused,
        out_shape=(
            jax.ShapeDtypeStruct((feats, width), BF16),
            jax.ShapeDtypeStruct((tokens, half), BF16),
        ),
        in_specs=[anyspace, anyspace, vmem, vmem, vmem, vmem],
        out_specs=(vmem, vmem),
        scratch_shapes=[
            pltpu.VMEM((width, width), F32),
            pltpu.VMEM((4, width // 4, width), F32),
            pltpu.VMEM((4, 16, width), F32),
            pltpu.VMEM((width, width), F32),
            pltpu.VMEM((4, width, width), BF16),
            pltpu.VMEM((8, width), F32),
            pltpu.VMEM((2, width, half), F32),
            pltpu.VMEM((8, tokens, width), BF16),
            pltpu.VMEM((width, tokens), BF16),
            pltpu.VMEM((4, 2, part, width), BF16),
            pltpu.VMEM((8, half, width), BF16),
            pltpu.VMEM((slots, tokens, half), BF16),
        ]
        + [
            pltpu.VMEM((2, width, half), BF16),
            pltpu.VMEM((2, width, half), BF16),
            pltpu.VMEM((width, half), BF16),
            pltpu.VMEM((width, half), BF16),
        ]
        * 2
        + [dma((4,))] * 8
        + [dma((8,))] * 2
        + [dma((16,))] * 2
        + [dma((4,))] * 8
        + [dma((6,))] * 2
        + [dma((slots + 1,))],
        compiler_params=pltpu.CompilerParams(
            collective_id=0, has_side_effects=True, vmem_limit_bytes=63 * 2**20
        ),
        cost_estimate=pl.CostEstimate(flops=20 * 10**9, bytes_accessed=30 * 10**6, transcendentals=0),
    )(
        hidden_in,
        proj_weight.reshape(2, 4, part, width),
        embed,
        embed_grad,
        eigvec,
        eigval.reshape(1, width),
    )


def solution(mesh):
    in_specs = (
        P("dp", None),
        P("dp", "chan"),
        P("dp", "chan"),
        P("dp", "chan"),
        P("chan", None),
        P("chan"),
    )
    out_specs = (P("dp", "chan"), P("dp", "chan"))
    small = mesh.shape["dp"] == 4 and mesh.shape["chan"] == 8
    run = local_fused if small else local
    return jax.shard_map(run, mesh=mesh, in_specs=in_specs, out_specs=out_specs, check_vma=False)
```

```python
import jax
import jax.numpy as jnp
from jax import lax
from jax.experimental import pallas as pl
from jax.experimental.pallas import tpu as pltpu
from jax.sharding import PartitionSpec as P

F32, BF16 = jnp.float32, jnp.bfloat16
HI = lax.Precision.HIGHEST
MID = lax.Precision.HIGH
MESH = pl.DeviceIdType.MESH


def dot(a, b, dims=((1,), (0,)), precision=None):
    return lax.dot_general(a, b, (dims, ((), ())), precision=precision, preferred_element_type=F32)


def pair(x):
    high = x.astype(BF16)
    return high, (x - high.astype(F32)).astype(BF16)


def local(hidden_in, proj_weight, embed, embed_grad, eigvec, eigval):
    rows = embed.shape[0] * lax.axis_size("dp")
    ones = jnp.ones((8, embed.shape[0]), BF16)
    sums_z, sums_g = dot(ones, embed), dot(ones, embed_grad)
    raw = dot(embed, embed_grad, ((0,), (0,)))
    packed = lax.psum(jnp.concatenate([raw, sums_z, sums_g], axis=0), "dp")
    width = raw.shape[0]
    raw = packed[:width]
    mean_z = packed[width : width + 1] / rows
    mean_g = packed[width + 8 : width + 9] / rows
    dmat = raw - rows * mean_z.T * mean_g
    sym = 0.5 * (dmat + dmat.T)
    root = jnp.sqrt(eigval)
    whiten = dot(eigvec / root[None, :], eigvec, ((1,), (1,)), MID)
    loewner = -1.0 / (root[:, None] * root[None, :] * (root[:, None] + root[None, :]))
    half_rot = dot(eigvec, sym, ((0,), (0,)), MID)
    rotated = dot(half_rot, eigvec, precision=MID)
    half_back = dot(eigvec, loewner * rotated, precision=MID)
    dsigma = dot(half_back, eigvec, ((1,), (1,)), MID) * (2.0 / rows)
    w_hi, w_lo = pair(whiten)
    d_hi, d_lo = pair(dsigma)
    shift = dot(mean_g, whiten, precision=HI) + dot(mean_z, dsigma, precision=HI)
    both = jnp.concatenate([embed_grad, embed], axis=1)
    grad_z = dot(both, jnp.concatenate([w_hi, d_hi], axis=0))
    grad_z += dot(both, jnp.concatenate([w_lo, d_lo], axis=0))
    grad_z = (grad_z - shift).astype(BF16)
    core = lax.rem(lax.axis_index("chan"), 2)
    size = lax.axis_size("chan")
    swap = [(k, k ^ 1) for k in range(size)]
    half = proj_weight.shape[0] // 2
    keep = lax.dynamic_slice_in_dim(proj_weight, core * half, half, 0)
    give = lax.dynamic_slice_in_dim(proj_weight, (1 - core) * half, half, 0)
    mate = lax.ppermute(give, "chan", swap)
    weights = jnp.concatenate([keep, mate], axis=1)
    weights = lax.all_gather(weights, "dp", axis=0, tiled=True)
    both_z = jnp.concatenate([grad_z, lax.ppermute(grad_z, "chan", swap)], axis=1)
    partial_input = dot(both_z, weights, ((1,), (1,))).astype(BF16)
    lines = [list(range(c, size, 2)) for c in range(2)]
    grad_hidden = lax.psum_scatter(
        partial_input, "chan", scatter_dimension=1, axis_index_groups=lines, tiled=True
    )
    partial_weight = dot(hidden_in, grad_z, ((0,), (0,))).astype(BF16)
    grad_weight = lax.psum_scatter(partial_weight, "dp", scatter_dimension=0, tiled=True)
    return (grad_weight, grad_hidden)


def dot3(a, b):
    a_hi, a_lo = pair(a)
    b_hi, b_lo = pair(b)
    return dot(a_hi, b_hi) + (dot(a_hi, b_lo) + dot(a_lo, b_hi))


def fused(
    hid, w4, z_ref, g_ref, u_ref, ev_ref, gw_ref, gh_ref,
    mom, mom_in, sums, dmat, sym_ref, mats, shift, acc_t, gz, gzt, wsc, wf, hb,
    a1s, a1r, a2s, a2r, b1s, b1r, b2s, b2r,
    mom_ss, mom_rs, sum_ss, sum_rs, dm_ss, dm_rs, w1_ss, w1_rs, w2_ss, w2_rs, wg_ss, wg_rs,
    rt_ss, rt_rs, lt_ss, lt_rs, sr_ss, sr_rs, sl_ss, sl_rs, red_ss, red_rs, loc,
):
    dp, chan = lax.axis_index("dp"), lax.axis_index("chan")
    px, py = lax.rem(dp, 2), dp // 2
    xn, yn, dg = 2 * py + (1 - px), 2 * (1 - py) + px, 2 * (1 - py) + (1 - px)
    zc, core = chan // 2, lax.rem(chan, 2)
    mate = 2 * zc + (1 - core)
    tokens, width = z_ref.shape
    rows = 4 * tokens
    quarter = width // 4
    part = wf.shape[1] // 4
    half = hb.shape[2]
    last = 3

    def plane(d):
        return lax.rem(dp + d, 4)

    def line(d):
        return lax.rem(chan + d, 8)

    def rdma(src, dst, ss, rs, where):
        return pltpu.make_async_remote_copy(
            src_ref=src, dst_ref=dst, send_sem=ss, recv_sem=rs, device_id=where, device_id_type=MESH
        )

    barrier = pltpu.get_barrier_semaphore()
    for d in range(1, 4):
        pl.semaphore_signal(barrier, inc=1, device_id={"dp": plane(d)}, device_id_type=MESH)
    for d in range(1, 8):
        pl.semaphore_signal(barrier, inc=1, device_id={"chan": line(d)}, device_id_type=MESH)

    order = [(dg, 0), (dg, 1), (xn, 0), (yn, 1), (yn, 0), (xn, 1), (dp, 0), (dp, 1)]
    slots = hb.shape[0]

    def fetch(n):
        block, side = order[n]
        start = pl.multiple_of(block * (2 * half) + side * half, half)
        return pltpu.make_async_copy(hid.at[:, pl.ds(start, half)], hb.at[n % slots], loc.at[n % slots])

    for n in range(slots):
        fetch(n).start()

    ones = jnp.ones((8, tokens), BF16)
    sums[dp, 0:8, :] = dot(ones, z_ref[...])
    sums[dp, 8:16, :] = dot(ones, g_ref[...])
    z_t = z_ref[...].astype(F32).T.astype(BF16)
    raw = dot(z_t, g_ref[...])
    raw = 0.5 * (raw + raw.T)
    mid = width // 2
    row_at = lax.broadcasted_iota(jnp.int32, (mid, mid), 0)
    col_at = lax.broadcasted_iota(jnp.int32, (mid, mid), 1)
    top = raw[:mid, :mid]
    diag = jnp.sum(jnp.where(row_at == col_at, top, 0.0), axis=0, keepdims=True)
    sums[dp, 16:24, :mid] = jnp.broadcast_to(diag, (8, mid))
    sums[dp, 16:24, mid:] = jnp.zeros((8, mid), F32)
    mom[:mid, :] = raw[:mid, mid:]
    mom[mid:, :] = jnp.where(row_at < col_at, top, raw[mid:, mid:])

    pl.semaphore_wait(barrier, 10)
    sends = []

    def go(copy):
        copy.start()
        sends.append(copy)
        return copy

    mom_c, sum_c, w1_c = [], [], []
    for d in range(1, 4):
        to = plane(d)
        where = {"dp": to}
        start = pl.multiple_of(to * quarter, quarter)
        mom_c.append(go(rdma(mom.at[pl.ds(start, quarter)], mom_in.at[d], mom_ss.at[d], mom_rs.at[d], where)))
        sum_c.append(go(rdma(sums.at[dp], sums.at[dp], sum_ss.at[d], sum_rs.at[d], where)))
    for d in range(1, 4):
        to = plane(d)
        w1_c.append(go(rdma(w4.at[:, to], wsc.at[dp], w1_ss.at[d], w1_rs.at[d], {"dp": to})))
    own_w = pltpu.make_async_copy(w4.at[:, dp], wsc.at[dp], loc.at[slots])
    own_w.start()

    u = u_ref[...]
    root_row = jnp.broadcast_to(jnp.sqrt(ev_ref[...]), (width, width))
    u_t = u.T
    whiten = dot3(u / root_row, u_t)
    mats[0], mats[1] = pair(whiten)
    root_col = root_row.T
    loewner = -1.0 / (root_row * root_col * (root_row + root_col))

    for c in mom_c:
        c.wait_recv()
    mine = pl.ds(pl.multiple_of(dp * quarter, quarter), quarter)
    dmat[mine, :] = (mom[mine, :] + mom_in[1]) + (mom_in[2] + mom_in[3])
    dm_c = []
    for d in range(1, 4):
        dm_c.append(go(rdma(dmat.at[mine], dmat.at[mine], dm_ss.at[d], dm_rs.at[d], {"dp": plane(d)})))
    for c in sum_c:
        c.wait_recv()
    for c in w1_c:
        c.wait_recv()
    own_w.wait()
    my_part = pl.ds(pl.multiple_of(dp * part, part), part)
    w2_c = []
    for d in range(1, 8):
        to = line(d)
        w2_c.append(
            go(
                rdma(
                    wsc.at[to // 2, lax.rem(to, 2)], wf.at[chan, my_part],
                    w2_ss.at[d], w2_rs.at[chan], {"chan": to},
                )
            )
        )
    own_w2 = pltpu.make_async_copy(wsc.at[zc, core], wf.at[chan, my_part], loc.at[slots])
    own_w2.start()

    to_x, to_y = {"dp": xn}, {"dp": yn}
    half_part = part // 2

    def landed(source):
        ref = wf.at[source, my_part]
        rdma(ref, ref, w2_ss.at[0], w2_rs.at[source], {"chan": mate}).wait_recv()

    paired = (zc, zc + 1 - 2 * lax.rem(zc, 2), lax.rem(zc + 2, 4), last - zc)

    def group(k):
        return pl.ds(2 * paired[k], 2)

    def spread(k):
        ref = wf.at[group(k), my_part]
        wg_c.append(
            [
                go(rdma(ref, ref, wg_ss.at[4 * n + k], wg_rs.at[4 * n + k], where))
                for n, where in enumerate((to_x, to_y))
            ]
        )

    def relay(k):
        ways = (
            (2, wg_c[k][1], yn * part, to_x),
            (3, wg_c[k][0], xn * part + half_part, to_y),
        )
        for n, arrived, start, where in ways:
            arrived.wait_recv()
            ref = wf.at[group(k), pl.ds(pl.multiple_of(start, half_part), half_part)]
            relay_c.append(go(rdma(ref, ref, wg_ss.at[4 * n + k], wg_rs.at[4 * n + k], where)))

    wg_c, relay_c = [], []
    own_w2.wait()
    landed(mate)
    spread(0)
    for c in dm_c:
        c.wait_recv()

    total = (sums[0] + sums[1]) + (sums[2] + sums[3])
    mean_z, mean_g = total[0:8] / rows, total[8:16] / rows
    cross, packed = dmat[:mid, :], dmat[mid:, :]
    flipped = packed.T
    diag = jnp.broadcast_to(total[16:17, :mid], (mid, mid))
    sym_ref[:mid, :mid] = jnp.where(
        row_at < col_at, packed, jnp.where(row_at == col_at, diag, flipped)
    )
    sym_ref[mid:, mid:] = jnp.where(row_at < col_at, flipped, packed)
    sym_ref[:mid, mid:] = cross
    sym_ref[mid:, :mid] = cross.T
    outer = jnp.broadcast_to(mean_z[0:1], (width, width)).T * mean_g[0:1]
    sym = sym_ref[...] - (0.5 * rows) * (outer + outer.T)
    rotated = dot3(dot3(u_t, sym), u)
    dsigma = dot3(dot3(u, loewner * rotated), u_t) * (2.0 / rows)
    mats[2], mats[3] = pair(dsigma)
    shift[...] = dot3(mean_g, whiten) + dot3(mean_z, dsigma)

    tile = tokens // 4

    @pl.loop(0, 4)
    def _(t):
        here = pl.ds(pl.multiple_of(t * tile, tile), tile)
        g, z = g_ref[here, :], z_ref[here, :]
        acc = (dot(g, mats[0]) + dot(z, mats[2])) + (dot(g, mats[1]) + dot(z, mats[3]))
        acc = acc - shift[0:1, :]
        gz[chan, here, :] = acc.astype(BF16)
        gzt[:, here] = acc.T.astype(BF16)

    def moves_right(k):
        slot = 2 * (zc - k) + core
        return rdma(gz.at[slot], gz.at[slot], rt_ss.at[k], rt_rs.at[k], {"chan": chan + 2})

    def moves_left(k):
        slot = 2 * (zc + k) + core
        return rdma(gz.at[slot], gz.at[slot], lt_ss.at[k], lt_rs.at[k], {"chan": chan - 2})

    def from_left(k):
        slot = 2 * (zc - 1 - k) + core
        return rdma(gz.at[slot], gz.at[slot], rt_ss.at[k], rt_rs.at[k], {"chan": chan - 2})

    def from_right(k):
        slot = 2 * (zc + 1 + k) + core
        return rdma(gz.at[slot], gz.at[slot], lt_ss.at[k], lt_rs.at[k], {"chan": chan + 2})

    def to_mate(block, ss, rs):
        slot = 2 * block + core
        return rdma(gz.at[slot], gz.at[slot], ss, rs, {"chan": mate})

    def has_left(k):
        return zc - 1 - k >= 0

    def has_right(k):
        return zc + 1 + k <= last

    def sends_right(k):
        return jnp.logical_and(zc - k >= 0, zc < last)

    def sends_left(k):
        return jnp.logical_and(zc + k <= last, zc > 0)

    def push(k):
        pl.when(sends_right(k))(lambda: moves_right(k).start())
        pl.when(sends_left(k))(lambda: moves_left(k).start())

    def take(k):
        @pl.when(has_left(k))
        def _():
            from_left(k).wait_recv()
            if k < 2:
                pl.when(zc < last)(lambda: moves_right(k + 1).start())
            to_mate(zc - 1 - k, sr_ss.at[k], sr_rs.at[k]).start()

        @pl.when(has_right(k))
        def _():
            from_right(k).wait_recv()
            if k < 2:
                pl.when(zc > 0)(lambda: moves_left(k + 1).start())
            to_mate(zc + 1 + k, sl_ss.at[k], sl_rs.at[k]).start()

    push(0)
    own_mate = go(to_mate(zc, sr_ss.at[3], sr_rs.at[3]))

    cols = half // 4

    def product(n, emit):
        fetch(n).wait()

        @pl.loop(0, 4)
        def _(t):
            here = pl.ds(pl.multiple_of(t * cols, cols), cols)
            emit(here, dot(gzt[...], hb[n % slots, :, here]))

        if n + slots < len(order):
            fetch(n + slots).start()

    def store(dst, idx):
        def emit(here, value):
            dst[idx, :, here] = value.astype(BF16)

        return emit

    product(0, store(a1s, 1))
    a1_dg = go(rdma(a1s.at[1], a1r.at[1], red_ss.at[0], red_rs.at[0], to_x))
    product(1, store(b1s, 1))
    b1_dg = go(rdma(b1s.at[1], b1r.at[1], red_ss.at[1], red_rs.at[1], to_y))

    def next_group(k):
        for c in range(2):
            landed(2 * paired[k] + c)
        spread(k)

    product(2, store(a1s, 0))
    a1_own = go(rdma(a1s.at[0], a1r.at[0], red_ss.at[2], red_rs.at[2], to_x))
    product(3, store(b1s, 0))
    b1_own = go(rdma(b1s.at[0], b1r.at[0], red_ss.at[3], red_rs.at[3], to_y))
    relay(0)
    take(0)

    def store_sum(dst, more):
        def emit(here, value):
            dst[:, here] = (value + more[1, :, here].astype(F32)).astype(BF16)

        return emit

    a1_dg.wait_recv()
    product(4, store_sum(a2s, a1r))
    a2 = go(rdma(a2s, a2r, red_ss.at[4], red_rs.at[4], to_y))
    b1_dg.wait_recv()
    product(5, store_sum(b2s, b1r))
    b2 = go(rdma(b2s, b2r, red_ss.at[5], red_rs.at[5], to_x))
    next_group(1)
    next_group(2)
    next_group(3)
    relay(1)
    take(1)

    def keep(side, first_in):
        def emit(here, value):
            acc_t[side, :, here] = value + first_in[0, :, here].astype(F32)

        return emit

    relay(2)
    a1_own.wait_recv()
    product(6, keep(0, a1r))
    b1_own.wait_recv()
    product(7, keep(1, b1r))
    relay(3)
    take(2)

    own_mate.wait_recv()
    for k in range(3):
        pl.when(has_left(k))(lambda k=k: to_mate(zc - 1 - k, sr_ss.at[k], sr_rs.at[k]).wait_recv())
        pl.when(has_right(k))(lambda k=k: to_mate(zc + 1 + k, sl_ss.at[k], sl_rs.at[k]).wait_recv())

    def hidden_part(owner):
        these = pl.ds(pl.multiple_of(owner * part, part), part)
        block = tokens // 2

        @pl.loop(0, 2)
        def _(t):
            here = pl.ds(pl.multiple_of(t * block, block), block)
            acc = dot(gz[0, here, :], wf[0, these, :], ((1,), (1,)))
            for e in range(1, 8):
                acc += dot(gz[e, here, :], wf[e, these, :], ((1,), (1,)))
            gh_ref[here, these] = acc.astype(BF16)

    hidden_part(dp)
    hidden_part(xn)
    hidden_part(yn)

    for side, arrived, ref in ((0, a2, a2r), (1, b2, b2r)):
        arrived.wait_recv()

        @pl.loop(0, 4)
        def _(t):
            start = pl.multiple_of(t * cols, cols)
            here = pl.ds(start, cols)
            value = acc_t[side, :, here] + ref[:, here].astype(F32)
            gw_ref[pl.ds(pl.multiple_of(side * half + start, cols), cols), :] = value.T.astype(BF16)

    for c in relay_c:
        c.wait_recv()
    hidden_part(dg)

    for c in sends:
        c.wait_send()
    for k in range(3):
        pl.when(sends_right(k))(lambda k=k: moves_right(k).wait_send())
        pl.when(sends_left(k))(lambda k=k: moves_left(k).wait_send())
        pl.when(has_left(k))(lambda k=k: to_mate(zc - 1 - k, sr_ss.at[k], sr_rs.at[k]).wait_send())
        pl.when(has_right(k))(lambda k=k: to_mate(zc + 1 + k, sl_ss.at[k], sl_rs.at[k]).wait_send())


def local_fused(hidden_in, proj_weight, embed, embed_grad, eigvec, eigval):
    tokens, width = embed.shape
    feats = proj_weight.shape[0]
    part, half = feats // 8, feats // 2
    vmem, anyspace = pl.BlockSpec(memory_space=pltpu.VMEM), pl.BlockSpec(memory_space=pl.ANY)
    dma = pltpu.SemaphoreType.DMA
    slots = 4
    return pl.pallas_call(
        fused,
        out_shape=(
            jax.ShapeDtypeStruct((feats, width), BF16),
            jax.ShapeDtypeStruct((tokens, half), BF16),
        ),
        in_specs=[anyspace, anyspace, vmem, vmem, vmem, vmem],
        out_specs=(vmem, vmem),
        scratch_shapes=[
            pltpu.VMEM((width, width // 2), F32),
            pltpu.VMEM((4, width // 4, width // 2), F32),
            pltpu.VMEM((4, 24, width), F32),
            pltpu.VMEM((width, width // 2), F32),
            pltpu.VMEM((width, width), F32),
            pltpu.VMEM((4, width, width), BF16),
            pltpu.VMEM((8, width), F32),
            pltpu.VMEM((2, width, half), F32),
            pltpu.VMEM((8, tokens, width), BF16),
            pltpu.VMEM((width, tokens), BF16),
            pltpu.VMEM((4, 2, part, width), BF16),
            pltpu.VMEM((8, half, width), BF16),
            pltpu.VMEM((slots, tokens, half), BF16),
        ]
        + [
            pltpu.VMEM((2, width, half), BF16),
            pltpu.VMEM((2, width, half), BF16),
            pltpu.VMEM((width, half), BF16),
            pltpu.VMEM((width, half), BF16),
        ]
        * 2
        + [dma((4,))] * 8
        + [dma((8,))] * 2
        + [dma((16,))] * 2
        + [dma((4,))] * 8
        + [dma((6,))] * 2
        + [dma((slots + 1,))],
        compiler_params=pltpu.CompilerParams(
            collective_id=0, has_side_effects=True, vmem_limit_bytes=63 * 2**20
        ),
        cost_estimate=pl.CostEstimate(flops=20 * 10**9, bytes_accessed=30 * 10**6, transcendentals=0),
    )(
        hidden_in,
        proj_weight.reshape(2, 4, part, width),
        embed,
        embed_grad,
        eigvec,
        eigval.reshape(1, width),
    )


def solution(mesh):
    in_specs = (
        P("dp", None),
        P("dp", "chan"),
        P("dp", "chan"),
        P("dp", "chan"),
        P("chan", None),
        P("chan"),
    )
    out_specs = (P("dp", "chan"), P("dp", "chan"))
    small = mesh.shape["dp"] == 4 and mesh.shape["chan"] == 8
    run = local_fused if small else local
    return jax.shard_map(run, mesh=mesh, in_specs=in_specs, out_specs=out_specs, check_vma=False)
```

```python
import jax
import jax.numpy as jnp
from jax import lax
from jax.experimental import pallas as pl
from jax.experimental.pallas import tpu as pltpu
from jax.sharding import PartitionSpec as P

F32, BF16 = jnp.float32, jnp.bfloat16
HI = lax.Precision.HIGHEST
MID = lax.Precision.HIGH
MESH = pl.DeviceIdType.MESH


def dot(a, b, dims=((1,), (0,)), precision=None):
    return lax.dot_general(a, b, (dims, ((), ())), precision=precision, preferred_element_type=F32)


def pair(x):
    high = x.astype(BF16)
    return high, (x - high.astype(F32)).astype(BF16)


def local(hidden_in, proj_weight, embed, embed_grad, eigvec, eigval):
    rows = embed.shape[0] * lax.axis_size("dp")
    ones = jnp.ones((8, embed.shape[0]), BF16)
    sums_z, sums_g = dot(ones, embed), dot(ones, embed_grad)
    raw = dot(embed, embed_grad, ((0,), (0,)))
    packed = lax.psum(jnp.concatenate([raw, sums_z, sums_g], axis=0), "dp")
    width = raw.shape[0]
    raw = packed[:width]
    mean_z = packed[width : width + 1] / rows
    mean_g = packed[width + 8 : width + 9] / rows
    dmat = raw - rows * mean_z.T * mean_g
    sym = 0.5 * (dmat + dmat.T)
    root = jnp.sqrt(eigval)
    whiten = dot(eigvec / root[None, :], eigvec, ((1,), (1,)), MID)
    loewner = -1.0 / (root[:, None] * root[None, :] * (root[:, None] + root[None, :]))
    half_rot = dot(eigvec, sym, ((0,), (0,)), MID)
    rotated = dot(half_rot, eigvec, precision=MID)
    half_back = dot(eigvec, loewner * rotated, precision=MID)
    dsigma = dot(half_back, eigvec, ((1,), (1,)), MID) * (2.0 / rows)
    w_hi, w_lo = pair(whiten)
    d_hi, d_lo = pair(dsigma)
    shift = dot(mean_g, whiten, precision=HI) + dot(mean_z, dsigma, precision=HI)
    both = jnp.concatenate([embed_grad, embed], axis=1)
    grad_z = dot(both, jnp.concatenate([w_hi, d_hi], axis=0))
    grad_z += dot(both, jnp.concatenate([w_lo, d_lo], axis=0))
    grad_z = (grad_z - shift).astype(BF16)
    core = lax.rem(lax.axis_index("chan"), 2)
    size = lax.axis_size("chan")
    swap = [(k, k ^ 1) for k in range(size)]
    half = proj_weight.shape[0] // 2
    keep = lax.dynamic_slice_in_dim(proj_weight, core * half, half, 0)
    give = lax.dynamic_slice_in_dim(proj_weight, (1 - core) * half, half, 0)
    mate = lax.ppermute(give, "chan", swap)
    weights = jnp.concatenate([keep, mate], axis=1)
    weights = lax.all_gather(weights, "dp", axis=0, tiled=True)
    both_z = jnp.concatenate([grad_z, lax.ppermute(grad_z, "chan", swap)], axis=1)
    partial_input = dot(both_z, weights, ((1,), (1,))).astype(BF16)
    lines = [list(range(c, size, 2)) for c in range(2)]
    grad_hidden = lax.psum_scatter(
        partial_input, "chan", scatter_dimension=1, axis_index_groups=lines, tiled=True
    )
    partial_weight = dot(hidden_in, grad_z, ((0,), (0,))).astype(BF16)
    grad_weight = lax.psum_scatter(partial_weight, "dp", scatter_dimension=0, tiled=True)
    return (grad_weight, grad_hidden)


def dot3(a, b):
    a_hi, a_lo = pair(a)
    b_hi, b_lo = pair(b)
    return dot(a_hi, b_hi) + (dot(a_hi, b_lo) + dot(a_lo, b_hi))


def fused(
    hid, w4, z_ref, g_ref, u_ref, ev_ref, gw_ref, gh_ref,
    mom, mom_in, sums, dmat, sym_ref, mats, shift, acc_t, gz, gzt, wsc, wf, hb,
    a1s, a1r, a2s, a2r, b1s, b1r, b2s, b2r,
    mom_ss, mom_rs, sum_ss, sum_rs, dm_ss, dm_rs, w1_ss, w1_rs, w2_ss, w2_rs, wg_ss, wg_rs,
    rt_ss, rt_rs, lt_ss, lt_rs, sr_ss, sr_rs, sl_ss, sl_rs, red_ss, red_rs, loc,
):
    dp, chan = lax.axis_index("dp"), lax.axis_index("chan")
    px, py = lax.rem(dp, 2), dp // 2
    xn, yn, dg = 2 * py + (1 - px), 2 * (1 - py) + px, 2 * (1 - py) + (1 - px)
    zc, core = chan // 2, lax.rem(chan, 2)
    mate = 2 * zc + (1 - core)
    tokens, width = z_ref.shape
    rows = 4 * tokens
    quarter = width // 4
    part = wf.shape[1] // 4
    half = hb.shape[2]
    last = 3

    def plane(d):
        return lax.rem(dp + d, 4)

    def line(d):
        return lax.rem(chan + d, 8)

    def rdma(src, dst, ss, rs, where):
        return pltpu.make_async_remote_copy(
            src_ref=src, dst_ref=dst, send_sem=ss, recv_sem=rs, device_id=where, device_id_type=MESH
        )

    barrier = pltpu.get_barrier_semaphore()
    for d in range(1, 4):
        pl.semaphore_signal(barrier, inc=1, device_id={"dp": plane(d)}, device_id_type=MESH)
    for d in range(1, 8):
        pl.semaphore_signal(barrier, inc=1, device_id={"chan": line(d)}, device_id_type=MESH)

    order = [(dg, 0), (dg, 1), (xn, 0), (yn, 1), (yn, 0), (xn, 1), (dp, 0), (dp, 1)]
    slots = hb.shape[0]

    def fetch(n):
        block, side = order[n]
        start = pl.multiple_of(block * (2 * half) + side * half, half)
        return pltpu.make_async_copy(hid.at[:, pl.ds(start, half)], hb.at[n % slots], loc.at[n % slots])

    for n in range(slots):
        fetch(n).start()

    ones = jnp.ones((8, tokens), BF16)
    sums[dp, 0:8, :] = dot(ones, z_ref[...])
    sums[dp, 8:16, :] = dot(ones, g_ref[...])
    z_t = z_ref[...].astype(F32).T.astype(BF16)
    raw = dot(z_t, g_ref[...])
    raw = 0.5 * (raw + raw.T)
    mid = width // 2
    row_at = lax.broadcasted_iota(jnp.int32, (mid, mid), 0)
    col_at = lax.broadcasted_iota(jnp.int32, (mid, mid), 1)
    top = raw[:mid, :mid]
    diag = jnp.sum(jnp.where(row_at == col_at, top, 0.0), axis=0, keepdims=True)
    sums[dp, 16:24, :mid] = jnp.broadcast_to(diag, (8, mid))
    sums[dp, 16:24, mid:] = jnp.zeros((8, mid), F32)
    mom[:mid, :] = raw[:mid, mid:]
    mom[mid:, :] = jnp.where(row_at < col_at, top, raw[mid:, mid:])

    pl.semaphore_wait(barrier, 10)
    sends = []

    def go(copy):
        copy.start()
        sends.append(copy)
        return copy

    mom_c, sum_c, w1_c = [], [], []
    for d in range(1, 4):
        to = plane(d)
        where = {"dp": to}
        start = pl.multiple_of(to * quarter, quarter)
        mom_c.append(go(rdma(mom.at[pl.ds(start, quarter)], mom_in.at[d], mom_ss.at[d], mom_rs.at[d], where)))
        sum_c.append(go(rdma(sums.at[dp], sums.at[dp], sum_ss.at[d], sum_rs.at[d], where)))
    u = u_ref[...]
    root_row = jnp.broadcast_to(jnp.sqrt(ev_ref[...]), (width, width))
    u_t = u.T
    whiten = dot3(u / root_row, u_t)
    mats[0], mats[1] = pair(whiten)
    root_col = root_row.T
    loewner = -1.0 / (root_row * root_col * (root_row + root_col))

    for c in mom_c:
        c.wait_recv()
    mine = pl.ds(pl.multiple_of(dp * quarter, quarter), quarter)
    dmat[mine, :] = (mom[mine, :] + mom_in[1]) + (mom_in[2] + mom_in[3])
    dm_c = []
    for d in range(1, 4):
        dm_c.append(go(rdma(dmat.at[mine], dmat.at[mine], dm_ss.at[d], dm_rs.at[d], {"dp": plane(d)})))
    for d in range(1, 4):
        to = plane(d)
        w1_c.append(go(rdma(w4.at[:, to], wsc.at[dp], w1_ss.at[d], w1_rs.at[d], {"dp": to})))
    own_w = pltpu.make_async_copy(w4.at[:, dp], wsc.at[dp], loc.at[slots])
    own_w.start()

    for c in sum_c:
        c.wait_recv()
    for c in dm_c:
        c.wait_recv()

    total = (sums[0] + sums[1]) + (sums[2] + sums[3])
    mean_z, mean_g = total[0:8] / rows, total[8:16] / rows
    cross, packed = dmat[:mid, :], dmat[mid:, :]
    flipped = packed.T
    diag = jnp.broadcast_to(total[16:17, :mid], (mid, mid))
    sym_ref[:mid, :mid] = jnp.where(
        row_at < col_at, packed, jnp.where(row_at == col_at, diag, flipped)
    )
    sym_ref[mid:, mid:] = jnp.where(row_at < col_at, flipped, packed)
    sym_ref[:mid, mid:] = cross
    sym_ref[mid:, :mid] = cross.T
    outer = jnp.broadcast_to(mean_z[0:1], (width, width)).T * mean_g[0:1]
    sym = sym_ref[...] - (0.5 * rows) * (outer + outer.T)
    rotated = dot3(dot3(u_t, sym), u)
    dsigma = dot3(dot3(u, loewner * rotated), u_t) * (2.0 / rows)
    mats[2], mats[3] = pair(dsigma)
    shift[...] = dot3(mean_g, whiten) + dot3(mean_z, dsigma)

    tile = tokens // 4

    @pl.loop(0, 4)
    def _(t):
        here = pl.ds(pl.multiple_of(t * tile, tile), tile)
        g, z = g_ref[here, :], z_ref[here, :]
        acc = (dot(g, mats[0]) + dot(z, mats[2])) + (dot(g, mats[1]) + dot(z, mats[3]))
        acc = acc - shift[0:1, :]
        gz[chan, here, :] = acc.astype(BF16)
        gzt[:, here] = acc.T.astype(BF16)

    def moves_right(k):
        slot = 2 * (zc - k) + core
        return rdma(gz.at[slot], gz.at[slot], rt_ss.at[k], rt_rs.at[k], {"chan": chan + 2})

    def moves_left(k):
        slot = 2 * (zc + k) + core
        return rdma(gz.at[slot], gz.at[slot], lt_ss.at[k], lt_rs.at[k], {"chan": chan - 2})

    def from_left(k):
        slot = 2 * (zc - 1 - k) + core
        return rdma(gz.at[slot], gz.at[slot], rt_ss.at[k], rt_rs.at[k], {"chan": chan - 2})

    def from_right(k):
        slot = 2 * (zc + 1 + k) + core
        return rdma(gz.at[slot], gz.at[slot], lt_ss.at[k], lt_rs.at[k], {"chan": chan + 2})

    def to_mate(block, ss, rs):
        slot = 2 * block + core
        return rdma(gz.at[slot], gz.at[slot], ss, rs, {"chan": mate})

    def has_left(k):
        return zc - 1 - k >= 0

    def has_right(k):
        return zc + 1 + k <= last

    def sends_right(k):
        return jnp.logical_and(zc - k >= 0, zc < last)

    def sends_left(k):
        return jnp.logical_and(zc + k <= last, zc > 0)

    def push(k):
        pl.when(sends_right(k))(lambda: moves_right(k).start())
        pl.when(sends_left(k))(lambda: moves_left(k).start())

    def take(k):
        @pl.when(has_left(k))
        def _():
            from_left(k).wait_recv()
            if k < 2:
                pl.when(zc < last)(lambda: moves_right(k + 1).start())
            to_mate(zc - 1 - k, sr_ss.at[k], sr_rs.at[k]).start()

        @pl.when(has_right(k))
        def _():
            from_right(k).wait_recv()
            if k < 2:
                pl.when(zc > 0)(lambda: moves_left(k + 1).start())
            to_mate(zc + 1 + k, sl_ss.at[k], sl_rs.at[k]).start()

    for c in w1_c:
        c.wait_recv()
    own_w.wait()
    my_part = pl.ds(pl.multiple_of(dp * part, part), part)
    w2_c = []
    for d in range(1, 8):
        to = line(d)
        w2_c.append(
            go(
                rdma(
                    wsc.at[to // 2, lax.rem(to, 2)], wf.at[chan, my_part],
                    w2_ss.at[d], w2_rs.at[chan], {"chan": to},
                )
            )
        )
    own_w2 = pltpu.make_async_copy(wsc.at[zc, core], wf.at[chan, my_part], loc.at[slots])
    own_w2.start()

    to_x, to_y = {"dp": xn}, {"dp": yn}
    half_part = part // 2

    def landed(source):
        ref = wf.at[source, my_part]
        rdma(ref, ref, w2_ss.at[0], w2_rs.at[source], {"chan": mate}).wait_recv()

    paired = (zc, zc + 1 - 2 * lax.rem(zc, 2), lax.rem(zc + 2, 4), last - zc)

    def group(k):
        return pl.ds(2 * paired[k], 2)

    def spread(k):
        ref = wf.at[group(k), my_part]
        wg_c.append(
            [
                go(rdma(ref, ref, wg_ss.at[4 * n + k], wg_rs.at[4 * n + k], where))
                for n, where in enumerate((to_x, to_y))
            ]
        )

    def relay(k):
        ways = (
            (2, wg_c[k][1], yn * part, to_x),
            (3, wg_c[k][0], xn * part + half_part, to_y),
        )
        for n, arrived, start, where in ways:
            arrived.wait_recv()
            ref = wf.at[group(k), pl.ds(pl.multiple_of(start, half_part), half_part)]
            relay_c.append(go(rdma(ref, ref, wg_ss.at[4 * n + k], wg_rs.at[4 * n + k], where)))

    wg_c, relay_c = [], []
    cols = half // 4

    def product(n, emit):
        fetch(n).wait()

        @pl.loop(0, 4)
        def _(t):
            here = pl.ds(pl.multiple_of(t * cols, cols), cols)
            emit(here, dot(gzt[...], hb[n % slots, :, here]))

        if n + slots < len(order):
            fetch(n + slots).start()

    def store(dst, idx):
        def emit(here, value):
            dst[idx, :, here] = value.astype(BF16)

        return emit

    product(0, store(a1s, 1))
    a1_dg = go(rdma(a1s.at[1], a1r.at[1], red_ss.at[0], red_rs.at[0], to_x))
    product(1, store(b1s, 1))
    b1_dg = go(rdma(b1s.at[1], b1r.at[1], red_ss.at[1], red_rs.at[1], to_y))

    def next_group(k):
        for c in range(2):
            landed(2 * paired[k] + c)
        spread(k)

    own_w2.wait()
    landed(mate)
    spread(0)
    product(2, store(a1s, 0))
    a1_own = go(rdma(a1s.at[0], a1r.at[0], red_ss.at[2], red_rs.at[2], to_x))
    product(3, store(b1s, 0))
    b1_own = go(rdma(b1s.at[0], b1r.at[0], red_ss.at[3], red_rs.at[3], to_y))
    push(0)
    own_mate = go(to_mate(zc, sr_ss.at[3], sr_rs.at[3]))

    relay(0)

    def store_sum(dst, more):
        def emit(here, value):
            dst[:, here] = (value + more[1, :, here].astype(F32)).astype(BF16)

        return emit

    a1_dg.wait_recv()
    product(4, store_sum(a2s, a1r))
    a2 = go(rdma(a2s, a2r, red_ss.at[4], red_rs.at[4], to_y))
    b1_dg.wait_recv()
    product(5, store_sum(b2s, b1r))
    b2 = go(rdma(b2s, b2r, red_ss.at[5], red_rs.at[5], to_x))
    take(0)
    next_group(1)
    next_group(2)
    next_group(3)
    relay(1)
    take(1)

    def keep(side, first_in):
        def emit(here, value):
            acc_t[side, :, here] = value + first_in[0, :, here].astype(F32)

        return emit

    relay(2)
    a1_own.wait_recv()
    product(6, keep(0, a1r))
    b1_own.wait_recv()
    product(7, keep(1, b1r))
    relay(3)
    take(2)

    own_mate.wait_recv()
    for k in range(3):
        pl.when(has_left(k))(lambda k=k: to_mate(zc - 1 - k, sr_ss.at[k], sr_rs.at[k]).wait_recv())
        pl.when(has_right(k))(lambda k=k: to_mate(zc + 1 + k, sl_ss.at[k], sl_rs.at[k]).wait_recv())

    def hidden_part(owner):
        these = pl.ds(pl.multiple_of(owner * part, part), part)
        block = tokens // 2

        @pl.loop(0, 2)
        def _(t):
            here = pl.ds(pl.multiple_of(t * block, block), block)
            acc = dot(gz[0, here, :], wf[0, these, :], ((1,), (1,)))
            for e in range(1, 8):
                acc += dot(gz[e, here, :], wf[e, these, :], ((1,), (1,)))
            gh_ref[here, these] = acc.astype(BF16)

    hidden_part(dp)
    hidden_part(xn)
    hidden_part(yn)

    for side, arrived, ref in ((0, a2, a2r), (1, b2, b2r)):
        arrived.wait_recv()

        @pl.loop(0, 4)
        def _(t):
            start = pl.multiple_of(t * cols, cols)
            here = pl.ds(start, cols)
            value = acc_t[side, :, here] + ref[:, here].astype(F32)
            gw_ref[pl.ds(pl.multiple_of(side * half + start, cols), cols), :] = value.T.astype(BF16)

    for c in relay_c:
        c.wait_recv()
    hidden_part(dg)

    for c in sends:
        c.wait_send()
    for k in range(3):
        pl.when(sends_right(k))(lambda k=k: moves_right(k).wait_send())
        pl.when(sends_left(k))(lambda k=k: moves_left(k).wait_send())
        pl.when(has_left(k))(lambda k=k: to_mate(zc - 1 - k, sr_ss.at[k], sr_rs.at[k]).wait_send())
        pl.when(has_right(k))(lambda k=k: to_mate(zc + 1 + k, sl_ss.at[k], sl_rs.at[k]).wait_send())


def local_fused(hidden_in, proj_weight, embed, embed_grad, eigvec, eigval):
    tokens, width = embed.shape
    feats = proj_weight.shape[0]
    part, half = feats // 8, feats // 2
    vmem, anyspace = pl.BlockSpec(memory_space=pltpu.VMEM), pl.BlockSpec(memory_space=pl.ANY)
    dma = pltpu.SemaphoreType.DMA
    slots = 4
    return pl.pallas_call(
        fused,
        out_shape=(
            jax.ShapeDtypeStruct((feats, width), BF16),
            jax.ShapeDtypeStruct((tokens, half), BF16),
        ),
        in_specs=[anyspace, anyspace, vmem, vmem, vmem, vmem],
        out_specs=(vmem, vmem),
        scratch_shapes=[
            pltpu.VMEM((width, width // 2), F32),
            pltpu.VMEM((4, width // 4, width // 2), F32),
            pltpu.VMEM((4, 24, width), F32),
            pltpu.VMEM((width, width // 2), F32),
            pltpu.VMEM((width, width), F32),
            pltpu.VMEM((4, width, width), BF16),
            pltpu.VMEM((8, width), F32),
            pltpu.VMEM((2, width, half), F32),
            pltpu.VMEM((8, tokens, width), BF16),
            pltpu.VMEM((width, tokens), BF16),
            pltpu.VMEM((4, 2, part, width), BF16),
            pltpu.VMEM((8, half, width), BF16),
            pltpu.VMEM((slots, tokens, half), BF16),
        ]
        + [
            pltpu.VMEM((2, width, half), BF16),
            pltpu.VMEM((2, width, half), BF16),
            pltpu.VMEM((width, half), BF16),
            pltpu.VMEM((width, half), BF16),
        ]
        * 2
        + [dma((4,))] * 8
        + [dma((8,))] * 2
        + [dma((16,))] * 2
        + [dma((4,))] * 8
        + [dma((6,))] * 2
        + [dma((slots + 1,))],
        compiler_params=pltpu.CompilerParams(
            collective_id=0, has_side_effects=True, vmem_limit_bytes=63 * 2**20
        ),
        cost_estimate=pl.CostEstimate(flops=20 * 10**9, bytes_accessed=30 * 10**6, transcendentals=0),
    )(
        hidden_in,
        proj_weight.reshape(2, 4, part, width),
        embed,
        embed_grad,
        eigvec,
        eigval.reshape(1, width),
    )


def solution(mesh):
    in_specs = (
        P("dp", None),
        P("dp", "chan"),
        P("dp", "chan"),
        P("dp", "chan"),
        P("chan", None),
        P("chan"),
    )
    out_specs = (P("dp", "chan"), P("dp", "chan"))
    small = mesh.shape["dp"] == 4 and mesh.shape["chan"] == 8
    run = local_fused if small else local
    return jax.shard_map(run, mesh=mesh, in_specs=in_specs, out_specs=out_specs, check_vma=False)
```

```python
import jax
import jax.numpy as jnp
from jax import lax
from jax.experimental import pallas as pl
from jax.experimental.pallas import tpu as pltpu
from jax.sharding import PartitionSpec as P

F32, BF16 = jnp.float32, jnp.bfloat16
HI = lax.Precision.HIGHEST
MID = lax.Precision.HIGH
MESH = pl.DeviceIdType.MESH


def dot(a, b, dims=((1,), (0,)), precision=None):
    return lax.dot_general(a, b, (dims, ((), ())), precision=precision, preferred_element_type=F32)


def pair(x):
    high = x.astype(BF16)
    return high, (x - high.astype(F32)).astype(BF16)


def local(hidden_in, proj_weight, embed, embed_grad, eigvec, eigval):
    rows = embed.shape[0] * lax.axis_size("dp")
    ones = jnp.ones((8, embed.shape[0]), BF16)
    sums_z, sums_g = dot(ones, embed), dot(ones, embed_grad)
    raw = dot(embed, embed_grad, ((0,), (0,)))
    packed = lax.psum(jnp.concatenate([raw, sums_z, sums_g], axis=0), "dp")
    width = raw.shape[0]
    raw = packed[:width]
    mean_z = packed[width : width + 1] / rows
    mean_g = packed[width + 8 : width + 9] / rows
    dmat = raw - rows * mean_z.T * mean_g
    sym = 0.5 * (dmat + dmat.T)
    root = jnp.sqrt(eigval)
    whiten = dot(eigvec / root[None, :], eigvec, ((1,), (1,)), MID)
    loewner = -1.0 / (root[:, None] * root[None, :] * (root[:, None] + root[None, :]))
    half_rot = dot(eigvec, sym, ((0,), (0,)), MID)
    rotated = dot(half_rot, eigvec, precision=MID)
    half_back = dot(eigvec, loewner * rotated, precision=MID)
    dsigma = dot(half_back, eigvec, ((1,), (1,)), MID) * (2.0 / rows)
    w_hi, w_lo = pair(whiten)
    d_hi, d_lo = pair(dsigma)
    shift = dot(mean_g, whiten, precision=HI) + dot(mean_z, dsigma, precision=HI)
    both = jnp.concatenate([embed_grad, embed], axis=1)
    grad_z = dot(both, jnp.concatenate([w_hi, d_hi], axis=0))
    grad_z += dot(both, jnp.concatenate([w_lo, d_lo], axis=0))
    grad_z = (grad_z - shift).astype(BF16)
    core = lax.rem(lax.axis_index("chan"), 2)
    size = lax.axis_size("chan")
    swap = [(k, k ^ 1) for k in range(size)]
    half = proj_weight.shape[0] // 2
    keep = lax.dynamic_slice_in_dim(proj_weight, core * half, half, 0)
    give = lax.dynamic_slice_in_dim(proj_weight, (1 - core) * half, half, 0)
    mate = lax.ppermute(give, "chan", swap)
    weights = jnp.concatenate([keep, mate], axis=1)
    weights = lax.all_gather(weights, "dp", axis=0, tiled=True)
    both_z = jnp.concatenate([grad_z, lax.ppermute(grad_z, "chan", swap)], axis=1)
    partial_input = dot(both_z, weights, ((1,), (1,))).astype(BF16)
    lines = [list(range(c, size, 2)) for c in range(2)]
    grad_hidden = lax.psum_scatter(
        partial_input, "chan", scatter_dimension=1, axis_index_groups=lines, tiled=True
    )
    partial_weight = dot(hidden_in, grad_z, ((0,), (0,))).astype(BF16)
    grad_weight = lax.psum_scatter(partial_weight, "dp", scatter_dimension=0, tiled=True)
    return (grad_weight, grad_hidden)


def dot3(a, b):
    a_hi, a_lo = pair(a)
    b_hi, b_lo = pair(b)
    return dot(a_hi, b_hi) + (dot(a_hi, b_lo) + dot(a_lo, b_hi))


def fused(
    hid, w4, z_ref, g_ref, u_ref, ev_ref, gw_ref, gh_ref,
    mom, mom_in, sums, dmat, sym_ref, mats, shift, acc_t, gz, gzt, wsc, wf, hb,
    a1s, a1r, a2s, a2r, b1s, b1r, b2s, b2r,
    mom_ss, mom_rs, sum_ss, sum_rs, dm_ss, dm_rs, w1_ss, w1_rs, w2_ss, w2_rs, wg_ss, wg_rs,
    rt_ss, rt_rs, lt_ss, lt_rs, sr_ss, sr_rs, sl_ss, sl_rs, red_ss, red_rs, loc,
):
    dp, chan = lax.axis_index("dp"), lax.axis_index("chan")
    px, py = lax.rem(dp, 2), dp // 2
    xn, yn, dg = 2 * py + (1 - px), 2 * (1 - py) + px, 2 * (1 - py) + (1 - px)
    zc, core = chan // 2, lax.rem(chan, 2)
    mate = 2 * zc + (1 - core)
    tokens, width = z_ref.shape
    rows = 4 * tokens
    quarter = width // 4
    part = wf.shape[1] // 4
    half = hb.shape[2]
    last = 3

    def plane(d):
        return lax.rem(dp + d, 4)

    def line(d):
        return lax.rem(chan + d, 8)

    def rdma(src, dst, ss, rs, where):
        return pltpu.make_async_remote_copy(
            src_ref=src, dst_ref=dst, send_sem=ss, recv_sem=rs, device_id=where, device_id_type=MESH
        )

    barrier = pltpu.get_barrier_semaphore()
    for d in range(1, 4):
        pl.semaphore_signal(barrier, inc=1, device_id={"dp": plane(d)}, device_id_type=MESH)
    for d in range(1, 8):
        pl.semaphore_signal(barrier, inc=1, device_id={"chan": line(d)}, device_id_type=MESH)

    order = [(dg, 0), (dg, 1), (xn, 0), (yn, 1), (yn, 0), (xn, 1), (dp, 0), (dp, 1)]
    slots = hb.shape[0]

    def fetch(n):
        block, side = order[n]
        start = pl.multiple_of(block * (2 * half) + side * half, half)
        return pltpu.make_async_copy(hid.at[:, pl.ds(start, half)], hb.at[n % slots], loc.at[n % slots])

    for n in range(slots):
        fetch(n).start()

    ones = jnp.ones((8, tokens), BF16)
    sums[dp, 0:8, :] = dot(ones, z_ref[...])
    sums[dp, 8:16, :] = dot(ones, g_ref[...])
    z_t = z_ref[...].astype(F32).T.astype(BF16)
    raw = dot(z_t, g_ref[...])
    raw = 0.5 * (raw + raw.T)
    mid = width // 2
    row_at = lax.broadcasted_iota(jnp.int32, (mid, mid), 0)
    col_at = lax.broadcasted_iota(jnp.int32, (mid, mid), 1)
    top = raw[:mid, :mid]
    diag = jnp.sum(jnp.where(row_at == col_at, top, 0.0), axis=0, keepdims=True)
    sums[dp, 16:24, :mid] = jnp.broadcast_to(diag, (8, mid))
    sums[dp, 16:24, mid:] = jnp.zeros((8, mid), F32)
    mom[:mid, :] = raw[:mid, mid:]
    mom[mid:, :] = jnp.where(row_at < col_at, top, raw[mid:, mid:])

    pl.semaphore_wait(barrier, 10)
    sends = []

    def go(copy):
        copy.start()
        sends.append(copy)
        return copy

    mom_c, sum_c, w1_c = [], [], []
    for d in range(1, 4):
        to = plane(d)
        where = {"dp": to}
        start = pl.multiple_of(to * quarter, quarter)
        mom_c.append(go(rdma(mom.at[pl.ds(start, quarter)], mom_in.at[d], mom_ss.at[d], mom_rs.at[d], where)))
        sum_c.append(go(rdma(sums.at[dp], sums.at[dp], sum_ss.at[d], sum_rs.at[d], where)))
    u = u_ref[...]
    root_row = jnp.broadcast_to(jnp.sqrt(ev_ref[...]), (width, width))
    u_t = u.T
    whiten = dot3(u / root_row, u_t)
    mats[0], mats[1] = pair(whiten)
    root_col = root_row.T
    loewner = -1.0 / (root_row * root_col * (root_row + root_col))

    for c in mom_c:
        c.wait_recv()
    mine = pl.ds(pl.multiple_of(dp * quarter, quarter), quarter)
    dmat[mine, :] = (mom[mine, :] + mom_in[1]) + (mom_in[2] + mom_in[3])
    dm_c = []
    for d in range(1, 4):
        dm_c.append(go(rdma(dmat.at[mine], dmat.at[mine], dm_ss.at[d], dm_rs.at[d], {"dp": plane(d)})))
    for d in range(1, 4):
        to = plane(d)
        w1_c.append(go(rdma(w4.at[:, to], wsc.at[dp], w1_ss.at[d], w1_rs.at[d], {"dp": to})))
    own_w = pltpu.make_async_copy(w4.at[:, dp], wsc.at[dp], loc.at[slots])
    own_w.start()

    for c in sum_c:
        c.wait_recv()
    for c in dm_c:
        c.wait_recv()

    total = (sums[0] + sums[1]) + (sums[2] + sums[3])
    mean_z, mean_g = total[0:8] / rows, total[8:16] / rows
    cross, packed = dmat[:mid, :], dmat[mid:, :]
    flipped = packed.T
    diag = jnp.broadcast_to(total[16:17, :mid], (mid, mid))
    sym_ref[:mid, :mid] = jnp.where(
        row_at < col_at, packed, jnp.where(row_at == col_at, diag, flipped)
    )
    sym_ref[mid:, mid:] = jnp.where(row_at < col_at, flipped, packed)
    sym_ref[:mid, mid:] = cross
    sym_ref[mid:, :mid] = cross.T
    outer = jnp.broadcast_to(mean_z[0:1], (width, width)).T * mean_g[0:1]
    sym = sym_ref[...] - (0.5 * rows) * (outer + outer.T)
    rotated = dot3(dot3(u_t, sym), u)
    dsigma = dot3(dot3(u, loewner * rotated), u_t) * (2.0 / rows)
    mats[2], mats[3] = pair(dsigma)
    shift[...] = dot3(mean_g, whiten) + dot3(mean_z, dsigma)

    tile = tokens // 4

    @pl.loop(0, 4)
    def _(t):
        here = pl.ds(pl.multiple_of(t * tile, tile), tile)
        g, z = g_ref[here, :], z_ref[here, :]
        acc = (dot(g, mats[0]) + dot(z, mats[2])) + (dot(g, mats[1]) + dot(z, mats[3]))
        acc = acc - shift[0:1, :]
        gz[chan, here, :] = acc.astype(BF16)
        gzt[:, here] = acc.T.astype(BF16)

    def moves_right(k):
        slot = 2 * (zc - k) + core
        return rdma(gz.at[slot], gz.at[slot], rt_ss.at[k], rt_rs.at[k], {"chan": chan + 2})

    def moves_left(k):
        slot = 2 * (zc + k) + core
        return rdma(gz.at[slot], gz.at[slot], lt_ss.at[k], lt_rs.at[k], {"chan": chan - 2})

    def from_left(k):
        slot = 2 * (zc - 1 - k) + core
        return rdma(gz.at[slot], gz.at[slot], rt_ss.at[k], rt_rs.at[k], {"chan": chan - 2})

    def from_right(k):
        slot = 2 * (zc + 1 + k) + core
        return rdma(gz.at[slot], gz.at[slot], lt_ss.at[k], lt_rs.at[k], {"chan": chan + 2})

    def to_mate(block, ss, rs):
        slot = 2 * block + core
        return rdma(gz.at[slot], gz.at[slot], ss, rs, {"chan": mate})

    def has_left(k):
        return zc - 1 - k >= 0

    def has_right(k):
        return zc + 1 + k <= last

    def sends_right(k):
        return jnp.logical_and(zc - k >= 0, zc < last)

    def sends_left(k):
        return jnp.logical_and(zc + k <= last, zc > 0)

    def push(k):
        pl.when(sends_right(k))(lambda: moves_right(k).start())
        pl.when(sends_left(k))(lambda: moves_left(k).start())

    def take(k):
        @pl.when(has_left(k))
        def _():
            from_left(k).wait_recv()
            if k < 2:
                pl.when(zc < last)(lambda: moves_right(k + 1).start())
            to_mate(zc - 1 - k, sr_ss.at[k], sr_rs.at[k]).start()

        @pl.when(has_right(k))
        def _():
            from_right(k).wait_recv()
            if k < 2:
                pl.when(zc > 0)(lambda: moves_left(k + 1).start())
            to_mate(zc + 1 + k, sl_ss.at[k], sl_rs.at[k]).start()

    for c in w1_c:
        c.wait_recv()
    own_w.wait()
    my_part = pl.ds(pl.multiple_of(dp * part, part), part)
    w2_c = []
    for d in range(1, 8):
        to = line(d)
        w2_c.append(
            go(
                rdma(
                    wsc.at[to // 2, lax.rem(to, 2)], wf.at[chan, my_part],
                    w2_ss.at[d], w2_rs.at[chan], {"chan": to},
                )
            )
        )
    own_w2 = pltpu.make_async_copy(wsc.at[zc, core], wf.at[chan, my_part], loc.at[slots])
    own_w2.start()

    push(0)
    own_mate = go(to_mate(zc, sr_ss.at[3], sr_rs.at[3]))

    to_x, to_y = {"dp": xn}, {"dp": yn}
    half_part = part // 2

    def landed(source):
        ref = wf.at[source, my_part]
        rdma(ref, ref, w2_ss.at[0], w2_rs.at[source], {"chan": mate}).wait_recv()

    paired = (zc, zc + 1 - 2 * lax.rem(zc, 2), lax.rem(zc + 2, 4), last - zc)

    def group(k):
        return pl.ds(2 * paired[k], 2)

    def spread(k):
        ref = wf.at[group(k), my_part]
        wg_c.append(
            [
                go(rdma(ref, ref, wg_ss.at[4 * n + k], wg_rs.at[4 * n + k], where))
                for n, where in enumerate((to_x, to_y))
            ]
        )

    def relay(k):
        ways = (
            (2, wg_c[k][1], yn * part, to_x),
            (3, wg_c[k][0], xn * part + half_part, to_y),
        )
        for n, arrived, start, where in ways:
            arrived.wait_recv()
            ref = wf.at[group(k), pl.ds(pl.multiple_of(start, half_part), half_part)]
            relay_c.append(go(rdma(ref, ref, wg_ss.at[4 * n + k], wg_rs.at[4 * n + k], where)))

    wg_c, relay_c = [], []
    cols = half // 4

    def product(n, emit):
        fetch(n).wait()

        @pl.loop(0, 4)
        def _(t):
            here = pl.ds(pl.multiple_of(t * cols, cols), cols)
            emit(here, dot(gzt[...], hb[n % slots, :, here]))

        if n + slots < len(order):
            fetch(n + slots).start()

    def store(dst, idx):
        def emit(here, value):
            dst[idx, :, here] = value.astype(BF16)

        return emit

    product(0, store(a1s, 1))
    a1_dg = go(rdma(a1s.at[1], a1r.at[1], red_ss.at[0], red_rs.at[0], to_x))
    product(1, store(b1s, 1))
    b1_dg = go(rdma(b1s.at[1], b1r.at[1], red_ss.at[1], red_rs.at[1], to_y))

    def next_group(k):
        for c in range(2):
            landed(2 * paired[k] + c)
        spread(k)

    own_w2.wait()
    landed(mate)
    spread(0)
    product(2, store(a1s, 0))
    a1_own = go(rdma(a1s.at[0], a1r.at[0], red_ss.at[2], red_rs.at[2], to_x))
    product(3, store(b1s, 0))
    b1_own = go(rdma(b1s.at[0], b1r.at[0], red_ss.at[3], red_rs.at[3], to_y))
    relay(0)

    def store_sum(dst, more):
        def emit(here, value):
            dst[:, here] = (value + more[1, :, here].astype(F32)).astype(BF16)

        return emit

    a1_dg.wait_recv()
    product(4, store_sum(a2s, a1r))
    a2 = go(rdma(a2s, a2r, red_ss.at[4], red_rs.at[4], to_y))
    b1_dg.wait_recv()
    product(5, store_sum(b2s, b1r))
    b2 = go(rdma(b2s, b2r, red_ss.at[5], red_rs.at[5], to_x))
    take(0)
    next_group(1)
    next_group(2)
    next_group(3)
    relay(1)
    take(1)

    def keep(side, first_in):
        def emit(here, value):
            acc_t[side, :, here] = value + first_in[0, :, here].astype(F32)

        return emit

    relay(2)
    a1_own.wait_recv()
    product(6, keep(0, a1r))
    b1_own.wait_recv()
    product(7, keep(1, b1r))
    relay(3)
    take(2)

    own_mate.wait_recv()
    for k in range(3):
        pl.when(has_left(k))(lambda k=k: to_mate(zc - 1 - k, sr_ss.at[k], sr_rs.at[k]).wait_recv())
        pl.when(has_right(k))(lambda k=k: to_mate(zc + 1 + k, sl_ss.at[k], sl_rs.at[k]).wait_recv())

    def hidden_part(owner):
        these = pl.ds(pl.multiple_of(owner * part, part), part)
        block = tokens // 2

        @pl.loop(0, 2)
        def _(t):
            here = pl.ds(pl.multiple_of(t * block, block), block)
            acc = dot(gz[0, here, :], wf[0, these, :], ((1,), (1,)))
            for e in range(1, 8):
                acc += dot(gz[e, here, :], wf[e, these, :], ((1,), (1,)))
            gh_ref[here, these] = acc.astype(BF16)

    hidden_part(dp)
    hidden_part(xn)
    hidden_part(yn)

    for side, arrived, ref in ((0, a2, a2r), (1, b2, b2r)):
        arrived.wait_recv()

        @pl.loop(0, 4)
        def _(t):
            start = pl.multiple_of(t * cols, cols)
            here = pl.ds(start, cols)
            value = acc_t[side, :, here] + ref[:, here].astype(F32)
            gw_ref[pl.ds(pl.multiple_of(side * half + start, cols), cols), :] = value.T.astype(BF16)

    these = pl.ds(pl.multiple_of(dg * part, part), part)
    block = tokens // 2

    def share(k, here):
        e = 2 * paired[k]
        value = dot(gz[e, here, :], wf[e, these, :], ((1,), (1,)))
        return value + dot(gz[e + 1, here, :], wf[e + 1, these, :], ((1,), (1,)))

    for c in relay_c[:6]:
        c.wait_recv()

    @pl.loop(0, 2)
    def _(t):
        here = pl.ds(pl.multiple_of(t * block, block), block)
        acc_t[t, :, :part] = share(0, here) + share(1, here) + share(2, here)

    for c in relay_c[6:]:
        c.wait_recv()

    @pl.loop(0, 2)
    def _(t):
        here = pl.ds(pl.multiple_of(t * block, block), block)
        gh_ref[here, these] = (acc_t[t, :, :part] + share(3, here)).astype(BF16)

    for c in sends:
        c.wait_send()
    for k in range(3):
        pl.when(sends_right(k))(lambda k=k: moves_right(k).wait_send())
        pl.when(sends_left(k))(lambda k=k: moves_left(k).wait_send())
        pl.when(has_left(k))(lambda k=k: to_mate(zc - 1 - k, sr_ss.at[k], sr_rs.at[k]).wait_send())
        pl.when(has_right(k))(lambda k=k: to_mate(zc + 1 + k, sl_ss.at[k], sl_rs.at[k]).wait_send())


def local_fused(hidden_in, proj_weight, embed, embed_grad, eigvec, eigval):
    tokens, width = embed.shape
    feats = proj_weight.shape[0]
    part, half = feats // 8, feats // 2
    vmem, anyspace = pl.BlockSpec(memory_space=pltpu.VMEM), pl.BlockSpec(memory_space=pl.ANY)
    dma = pltpu.SemaphoreType.DMA
    slots = 4
    return pl.pallas_call(
        fused,
        out_shape=(
            jax.ShapeDtypeStruct((feats, width), BF16),
            jax.ShapeDtypeStruct((tokens, half), BF16),
        ),
        in_specs=[anyspace, anyspace, vmem, vmem, vmem, vmem],
        out_specs=(vmem, vmem),
        scratch_shapes=[
            pltpu.VMEM((width, width // 2), F32),
            pltpu.VMEM((4, width // 4, width // 2), F32),
            pltpu.VMEM((4, 24, width), F32),
            pltpu.VMEM((width, width // 2), F32),
            pltpu.VMEM((width, width), F32),
            pltpu.VMEM((4, width, width), BF16),
            pltpu.VMEM((8, width), F32),
            pltpu.VMEM((2, width, half), F32),
            pltpu.VMEM((8, tokens, width), BF16),
            pltpu.VMEM((width, tokens), BF16),
            pltpu.VMEM((4, 2, part, width), BF16),
            pltpu.VMEM((8, half, width), BF16),
            pltpu.VMEM((slots, tokens, half), BF16),
        ]
        + [
            pltpu.VMEM((2, width, half), BF16),
            pltpu.VMEM((2, width, half), BF16),
            pltpu.VMEM((width, half), BF16),
            pltpu.VMEM((width, half), BF16),
        ]
        * 2
        + [dma((4,))] * 8
        + [dma((8,))] * 2
        + [dma((16,))] * 2
        + [dma((4,))] * 8
        + [dma((6,))] * 2
        + [dma((slots + 1,))],
        compiler_params=pltpu.CompilerParams(
            collective_id=0, has_side_effects=True, vmem_limit_bytes=63 * 2**20
        ),
        cost_estimate=pl.CostEstimate(flops=20 * 10**9, bytes_accessed=30 * 10**6, transcendentals=0),
    )(
        hidden_in,
        proj_weight.reshape(2, 4, part, width),
        embed,
        embed_grad,
        eigvec,
        eigval.reshape(1, width),
    )


def solution(mesh):
    in_specs = (
        P("dp", None),
        P("dp", "chan"),
        P("dp", "chan"),
        P("dp", "chan"),
        P("chan", None),
        P("chan"),
    )
    out_specs = (P("dp", "chan"), P("dp", "chan"))
    small = mesh.shape["dp"] == 4 and mesh.shape["chan"] == 8
    run = local_fused if small else local
    return jax.shard_map(run, mesh=mesh, in_specs=in_specs, out_specs=out_specs, check_vma=False)
```
